256 devices in a mesh: queue: 32 (over x, y, core), seq: 8 (over z).
Axes of the slice: x: 4, y: 4, z: 8, core: 2. Of those that a mesh axis runs over, the one named last changes fastest.
Arguments:
- hidden: bfloat16 [256, 64, 3072], P('seq', 'queue'), may hold values from -6 to 6
- latent: bfloat16 [256, 64, 64], P('seq', 'queue'), may hold values from -6 to 6
- fresh_noise: bfloat16 [256, 64], P('seq'), may hold values from -6 to 6
- timesteps: int32 [64], P('queue'), may hold values from 16 to 1039, as said below
- queue_slots: int32 [64], replicated, may hold values from 0 to 127, as said below
- windows: int32 [64], replicated, may hold values from 1 to 2, as said below
- mod_weight: bfloat16 [3, 128, 3072], P(None, None, 'seq'), may hold values from -0.5 to 0.5
- attention_weight: bfloat16 [3072, 12288], P(None, 'seq')
- final_weight: bfloat16 [3072, 64], replicated, may hold values from -0.109375 to 0.109375
Outputs:
- block_out: bfloat16 [256, 64, 3072], P('seq', 'queue')
- noise_pred: bfloat16 [256, 64, 64], P('seq', 'queue')
- new_queue: bfloat16 [256, 64, 64], P('seq', 'queue')
The draws below stay inside these ranges and needn't reach their ends.
Inputs may be any that keep to these rules, and one draw needn't show every extreme that they name: `timesteps`: frame f has a timestep from (f + 1) * 16 to (f + 2) * 16 - 1. `queue_slots`: frame f has the slot 2 f or 2 f + 1; the first frame has slot 0 and the last the slot 127. `windows`: some frame has a window of 2.
All inputs are finite; a program needn't handle non-finite values.
Results may differ from the reference program's by a relative error of at most 0.02.
Values may be sent and summed in bfloat16 or wider, within the bound.
A program may use at most 128 MiB of HBM per device.

```python
import math
import jax
import jax.numpy as jnp
from jax import lax

D = 3072
HEADS = 24
HD = 128
FREQ = 128
LAT = 64
STRIDE = 16
WMAX = 2
FRAMES = 64
FRAME_TOK = 256


def draw_timesteps(key, part):
    key = jax.random.fold_in(key, 11)
    offsets = jax.random.randint(key, (FRAMES,), 0, STRIDE)
    offsets = offsets.at[0].set(0).at[FRAMES - 1].set(STRIDE - 1)
    return ((jnp.arange(FRAMES, dtype=jnp.int32) + 1) * STRIDE + offsets).astype(jnp.int32)


def draw_queue_slots(key, part):
    key = jax.random.fold_in(key, 12)
    offsets = jax.random.randint(key, (FRAMES,), 0, 2)
    offsets = offsets.at[0].set(0).at[FRAMES - 1].set(1)
    return (2 * jnp.arange(FRAMES, dtype=jnp.int32) + offsets).astype(jnp.int32)


def draw_windows(key, part):
    key = jax.random.fold_in(key, 13)
    size_key, spot_key = jax.random.split(key)
    window_sizes = jax.random.randint(size_key, (FRAMES,), 1, WMAX + 1)
    chosen = jax.random.randint(spot_key, (), 0, FRAMES)
    return window_sizes.at[chosen].set(WMAX).astype(jnp.int32)


def draw_attention_weight(key, part):
    key = jax.random.fold_in(key, 14)
    entries = jax.random.normal(key, (D, HEADS, 4, HD), jnp.float32) * D ** (-0.5)
    queries = entries[:, :, 0]
    key_cols = entries[:, :, 1]
    stacked = jnp.stack([queries, key_cols, entries[:, :, 2], entries[:, :, 3] * 2.0], axis=2)
    return stacked.reshape(D, 4 * D).astype(jnp.bfloat16)


def levels(rng, dims, pieces, low, largest):
    gain = 1.0
    for position, shards_of in pieces:
        steps = jax.random.uniform(jax.random.fold_in(jax.random.fold_in(rng, 6), position), (shards_of,), jnp.float32, low / len(pieces), largest / len(pieces))
        gain = gain * jnp.repeat(jnp.exp(steps), dims[position] // shards_of).reshape((-1,) + (1,) * (len(dims) - 1 - position))
    return gain


def bell_draw(rng, shape, scale, bound, pieces=(), kind=jnp.bfloat16):
    values = scale * jax.random.normal(rng, shape, jnp.float32)
    if pieces:
        values = values * levels(rng, shape, pieces, -0.22, 0.18)
    return jnp.clip(values, -bound, bound).astype(kind)


def setup_inputs(seed: int = 0) -> dict:
    splits = jax.random.split(jax.random.key(seed), 10)
    return {
        "hidden": bell_draw(splits[0], (FRAME_TOK, FRAMES, D), 1.0, 6.0, ((0, 8), (1, 32))),
        "latent": bell_draw(splits[1], (FRAME_TOK, FRAMES, LAT), 1.0, 6.0, ((0, 8), (1, 32))),
        "fresh_noise": bell_draw(splits[2], (FRAME_TOK, LAT), 1.0, 6.0, ((0, 8),)),
        "timesteps": draw_timesteps(jax.random.fold_in(splits[9], 71), 0),
        "queue_slots": draw_queue_slots(jax.random.fold_in(splits[9], 71), 0),
        "windows": draw_windows(jax.random.fold_in(splits[9], 71), 0),
        "mod_weight": bell_draw(splits[6], (3, FREQ, D), FREQ ** -0.5, 0.5, ((2, 8),)),
        "attention_weight": draw_attention_weight(jax.random.fold_in(splits[9], 71), 0),
        "final_weight": bell_draw(splits[8], (D, LAT), D ** -0.5, 0.109375),
    }


LN_EPS = 1e-06
DECAY = 2.3
NEAR_COST = 0.5

def frequencies(timestep_ids, embed_width):
    half_width = embed_width // 2
    ladder = jnp.exp(jnp.arange(half_width, dtype=jnp.float32) * (-math.log(10000.0) / half_width))
    angles = timestep_ids.astype(jnp.float32)[:, None] * ladder[None, :]
    return jnp.concatenate([jnp.cos(angles), jnp.sin(angles)], axis=1)

def plan(timestep_ids, horizon):
    return jnp.exp(timestep_ids.astype(jnp.float32) * (-DECAY / horizon))

def denoise(latent_now, noise_term, timestep_ids, horizon):
    alpha_now = plan(timestep_ids, horizon)
    before = plan(timestep_ids - STRIDE, horizon)
    clean_part = (latent_now - jnp.sqrt(1.0 - alpha_now) * noise_term) / jnp.sqrt(alpha_now)
    return jnp.sqrt(before) * clean_part + jnp.sqrt(1.0 - before) * noise_term

def spatial(queries, key_rows, value_rows):
    factor = 1.0 / math.sqrt(queries.shape[-1])
    scores = jnp.einsum('qhe,khe->hqk', queries.astype(jnp.float32), key_rows.astype(jnp.float32)) * factor
    peak = lax.optimization_barrier(jnp.max(scores, axis=2, keepdims=True))
    expo_terms = jnp.exp(scores - peak)
    denominator = lax.optimization_barrier(jnp.sum(expo_terms, axis=2))
    rounded = lax.optimization_barrier(expo_terms.astype(jnp.bfloat16))
    combined = jnp.einsum('hqk,khe->qhe', rounded.astype(jnp.float32), value_rows.astype(jnp.float32))
    return combined / jnp.transpose(denominator)[:, :, None]

def temporal(queries, keys_pad, values_pad, first_frame, queue_slots, windows):
    frames_here = queries.shape[1]
    reach_span = 2 * WMAX + 1
    frame_total = queue_slots.shape[0]
    factor = 1.0 / math.sqrt(queries.shape[-1])
    near_keys = jnp.stack([keys_pad[:, offset:offset + frames_here] for offset in range(reach_span)], axis=2)
    near_values = jnp.stack([values_pad[:, offset:offset + frames_here] for offset in range(reach_span)], axis=2)
    scores = jnp.einsum('rihe,ridhe->ridh', queries.astype(jnp.float32), near_keys.astype(jnp.float32)) * factor
    padded_slots = jnp.pad(queue_slots, (WMAX, WMAX))
    nearby = lax.dynamic_slice_in_dim(padded_slots, first_frame, frames_here + 2 * WMAX, 0)
    near_slots = jnp.stack([nearby[offset:offset + frames_here] for offset in range(reach_span)], axis=1)
    own_slot = lax.dynamic_slice_in_dim(queue_slots, first_frame, frames_here, 0)
    frame_reach = lax.dynamic_slice_in_dim(windows, first_frame, frames_here, 0)
    frame_index = first_frame + jnp.arange(frames_here, dtype=jnp.int32)[:, None] + jnp.arange(reach_span, dtype=jnp.int32)[None, :] - WMAX
    slot_gap = jnp.abs(near_slots - own_slot[:, None])
    allowed = (frame_index >= 0) & (frame_index < frame_total) & (slot_gap <= frame_reach[:, None])
    logits = scores - NEAR_COST * slot_gap.astype(jnp.float32)[None, :, :, None]
    inside = allowed[None, :, :, None]
    peak = lax.optimization_barrier(jnp.max(jnp.where(inside, logits, -1e+30), axis=2, keepdims=True))
    weights = jnp.where(inside, jnp.exp(jnp.where(inside, logits, peak) - peak), 0.0)
    summed = lax.optimization_barrier(jnp.sum(weights, axis=2))
    combined = jnp.einsum('ridh,ridhe->rihe', weights, near_values.astype(jnp.float32))
    return combined / summed[..., None]

def reference(hidden, latent, fresh_noise, timesteps, queue_slots, windows, mod_weight, attention_weight, final_weight):
    horizon = STRIDE * (FRAMES + 1)
    embedded = lax.optimization_barrier(jax.nn.silu(frequencies(timesteps, FREQ)).astype(jnp.bfloat16))
    modulation = jnp.einsum('fk,pkd->pfd', embedded.astype(jnp.float32), mod_weight.astype(jnp.float32))
    values = hidden.astype(jnp.float32)
    centred = values - lax.optimization_barrier(jnp.mean(values, axis=2, keepdims=True))
    variance = lax.optimization_barrier(jnp.mean(centred * centred, axis=2, keepdims=True))
    normal = (centred * lax.rsqrt(variance + LN_EPS) * (1.0 + modulation[1][None]) + modulation[0][None]).astype(jnp.bfloat16)
    layout = attention_weight.reshape(D, HEADS, 4, HD)
    qkv_weight = layout[:, :, :3, :].reshape(D, HEADS * 3 * HD)
    out_weight = layout[:, :, 3, :].reshape(D, D)
    frame_ids = jnp.arange(FRAMES, dtype=jnp.int32)

    def project(frame):
        token_rows = lax.dynamic_index_in_dim(normal, frame, 1, keepdims=False)
        product = jnp.dot(token_rows, qkv_weight, preferred_element_type=jnp.float32)
        return lax.optimization_barrier(product.astype(jnp.bfloat16)).reshape(FRAME_TOK, HEADS, 3, HD)
    projected = lax.map(project, frame_ids)
    edge = ((WMAX, WMAX), (0, 0), (0, 0), (0, 0))
    key_pad = jnp.pad(projected[:, :, :, 1, :], edge)
    value_pad = jnp.pad(projected[:, :, :, 2, :], edge)

    def one_frame(frame):
        triple = lax.dynamic_index_in_dim(projected, frame, 0, keepdims=False)
        queries = triple[:, :, 0]
        spread = spatial(queries, triple[:, :, 1], triple[:, :, 2])
        near_keys = jnp.moveaxis(lax.dynamic_slice_in_dim(key_pad, frame, 2 * WMAX + 1, 0), 0, 1)
        near_values = jnp.moveaxis(lax.dynamic_slice_in_dim(value_pad, frame, 2 * WMAX + 1, 0), 0, 1)
        along = temporal(queries[:, None], near_keys, near_values, frame, queue_slots, windows)[:, 0]
        heads = (spread + along).astype(jnp.bfloat16).reshape(FRAME_TOK, D)
        combined = jnp.dot(heads, jnp.transpose(out_weight), preferred_element_type=jnp.float32)
        gate_row = lax.dynamic_index_in_dim(modulation[2], frame, 0, keepdims=False)
        residual = lax.dynamic_index_in_dim(hidden, frame, 1, keepdims=False).astype(jnp.float32)
        block_rows = (residual + gate_row[None] * combined).astype(jnp.bfloat16)
        noise_term = jnp.dot(block_rows, final_weight, preferred_element_type=jnp.float32)
        latent_rows = lax.dynamic_index_in_dim(latent, frame, 1, keepdims=False).astype(jnp.float32)
        step_id = lax.dynamic_index_in_dim(timesteps, frame, 0, keepdims=False)
        updated = denoise(latent_rows, noise_term, step_id, horizon).astype(jnp.bfloat16)
        return (block_rows, noise_term.astype(jnp.bfloat16), updated)
    block_rows, noise_rows, updated = lax.map(one_frame, frame_ids)
    block_out = jnp.transpose(block_rows, (1, 0, 2))
    noise_pred = jnp.transpose(noise_rows, (1, 0, 2))
    moved = jnp.transpose(updated, (1, 0, 2))
    new_queue = jnp.concatenate([moved[:, 1:], fresh_noise[:, None]], axis=1)
    return (block_out, noise_pred, new_queue)
```

```python
import functools
import math

import jax
import jax.numpy as jnp
from jax import lax
from jax.experimental import pallas as pl
from jax.experimental.pallas import tpu as pltpu
from jax.sharding import PartitionSpec as P

HD = 128
STRIDE = 16
WMAX = 2

LN_EPS = 1e-06
DECAY = 2.3
NEAR_COST = 0.5

MESH = pl.DeviceIdType.MESH
F32 = jnp.float32
BF16 = jnp.bfloat16
NT = (((1,), (1,)), ((), ()))


def kernel(
    Q,
    Z,
    hid,
    lat,
    fresh,
    steps,
    slots,
    wins,
    mw_hbm,
    w_hbm,
    fw_hbm,
    out,
    pred,
    queue,
    xs,
    wqkv,
    wout,
    mw,
    fw,
    part,
    mod,
    norm,
    qb,
    kv,
    hd,
    sent_r,
    sent_l,
    in_r,
    in_l,
    upd,
    got,
    w_sem,
    mw_sem,
    fw_sem,
    mod_send,
    mod_recv,
    ag_send,
    ag_recv,
    halo_send,
    halo_recv,
    rs_send,
    rs_recv,
    edge_send,
    edge_recv,
):
    F, T, D = hid.shape
    LH = w_hbm.shape[1] // (4 * HD)
    MP = mw_hbm.shape[2]
    FREQ = mw_hbm.shape[1]
    FRAMES = F * Q
    factor = 1.0 / math.sqrt(HD)
    z = lax.axis_index("seq")
    q = lax.axis_index("queue")
    z_right, z_left = lax.rem(z + 1, Z), lax.rem(z + Z - 1, Z)
    q_right, q_left = lax.rem(q + 1, Q), lax.rem(q + Q - 1, Q)

    def weight_copies():
        copies = []
        for h in range(LH):
            copies.append(
                pltpu.make_async_copy(
                    w_hbm.at[:, pl.ds(h * 4 * HD, 3 * HD)],
                    wqkv.at[:, pl.ds(h * 3 * HD, 3 * HD)],
                    w_sem.at[h],
                )
            )
        for h in range(LH):
            copies.append(
                pltpu.make_async_copy(
                    w_hbm.at[:, pl.ds(h * 4 * HD + 3 * HD, HD)],
                    wout.at[:, pl.ds(h * HD, HD)],
                    w_sem.at[LH + h],
                )
            )
        return copies

    weights = weight_copies()
    mw_copy = pltpu.make_async_copy(mw_hbm, mw, mw_sem)
    fw_copy = pltpu.make_async_copy(fw_hbm, fw, fw_sem)
    mw_copy.start()
    for copy in weights:
        copy.start()
    fw_copy.start()

    barrier = pltpu.get_barrier_semaphore()
    for k in range(1, Z):
        pl.semaphore_signal(
            barrier, inc=1, device_id=(q, lax.rem(z + k, Z)), device_id_type=MESH
        )
    for other in (q_left, q_right):
        pl.semaphore_signal(barrier, inc=1, device_id=(other, z), device_id_type=MESH)
    pl.semaphore_wait(barrier, Z + 1)

    def gather_copy(way, u, src, chunk, frame):
        return pltpu.make_async_remote_copy(
            src_ref=src,
            dst_ref=xs.at[chunk, frame],
            send_sem=ag_send.at[way, u],
            recv_sem=ag_recv.at[way, u],
            device_id=(q, z_right if way == 0 else z_left),
            device_id_type=MESH,
        )

    for u in (1, 2):
        gather_copy(0, u, hid.at[u - 1], z, u - 1).start()
        gather_copy(1, u, hid.at[2 - u], z, 2 - u).start()

    xs[z] = hid[...]
    for slot in (0, 1):
        in_r[slot] = jnp.zeros((T, D), BF16)
        in_l[slot] = jnp.zeros((T, D), BF16)

    rows = lax.broadcasted_iota(jnp.int32, (8, FREQ), 0)
    lanes = lax.broadcasted_iota(jnp.int32, (8, FREQ), 1)
    half = FREQ // 2
    ladder = jnp.exp(lax.rem(lanes, half).astype(F32) * (-math.log(10000.0) / half))
    ids = jnp.where(lax.rem(rows, 2) == 0, steps[0], steps[1])
    angles = ids.astype(F32) * ladder
    freq = jnp.where(lanes < half, jnp.cos(angles), jnp.sin(angles))
    temb = (freq / (1.0 + jnp.exp(-freq))).astype(BF16)
    mw_copy.wait()
    rows = lax.broadcasted_iota(jnp.int32, (8, MP), 0)
    maps = [jnp.dot(temb, mw[p], preferred_element_type=F32) for p in range(3)]
    part[...] = jnp.where(rows < 2, maps[0], jnp.where(rows < 4, maps[1], maps[2]))

    def mod_copy(k, owner):
        return pltpu.make_async_remote_copy(
            src_ref=part,
            dst_ref=mod.at[:, pl.ds(pl.multiple_of(owner * MP, MP), MP)],
            send_sem=mod_send.at[k],
            recv_sem=mod_recv.at[k],
            device_id=(q, lax.rem(z + k, Z)),
            device_id_type=MESH,
        )

    for k in range(1, Z):
        mod_copy(k, z).start()
    mod[:, pl.ds(pl.multiple_of(z * MP, MP), MP)] = part[...]
    for k in range(1, Z):
        mod_copy(k, lax.rem(z + Z - k, Z)).wait_recv()
    for copy in weights:
        copy.wait()

    def normalise(chunk, frame, base):
        scale = 1.0 + mod[pl.ds(2 + frame, 1), :]
        shift = mod[pl.ds(frame, 1), :]
        for r in range(0, T, 16):
            x = xs[chunk, frame, r : r + 16, :].astype(F32)
            centred = x - jnp.sum(x, axis=1, keepdims=True) * (1.0 / D)
            variance = jnp.sum(centred * centred, axis=1, keepdims=True) * (1.0 / D)
            y = centred * lax.rsqrt(variance + LN_EPS) * scale + shift
            norm[base + r : base + r + 16, :] = y.astype(BF16)

    def halo_copy(side, u, i, chunk, frame):
        rows_here = pl.ds(pl.multiple_of(chunk * T, T), T)
        return pltpu.make_async_remote_copy(
            src_ref=kv.at[F + frame, rows_here],
            dst_ref=kv.at[frame + (0 if side == 0 else 2 * F), rows_here],
            send_sem=halo_send.at[side, i, u],
            recv_sem=halo_recv.at[side, i, u],
            device_id=(q_right if side == 0 else q_left, z),
            device_id_type=MESH,
        )

    def gather_place(u):
        step = (u + 1) // 2
        left = (lax.rem(z + Z - step, Z), lax.rem(u + 1, 2))
        right = (lax.rem(z + step, Z), lax.rem(u, 2))
        return left, right

    def gather_unit(u, carry):
        places = gather_place(u)

        @pl.when(u >= 1)
        def _():
            for way in (0, 1):
                chunk, frame = places[way]
                gather_copy(way, u, xs.at[chunk, frame], chunk, frame).wait_recv()

                @pl.when(u + 2 <= Z - 1)
                def _():
                    gather_copy(way, u + 2, xs.at[chunk, frame], chunk, frame).start()

        for way in (0, 1):
            normalise(*places[way], way * T)
        projected = jnp.dot(norm[...], wqkv[...], preferred_element_type=F32).astype(BF16)
        for way in (0, 1):
            chunk, frame = places[way]
            rows_here = pl.ds(pl.multiple_of(chunk * T, T), T)
            block = projected[way * T : (way + 1) * T]
            for h in range(LH):
                at = h * 3 * HD
                qb[frame, rows_here, h * HD : (h + 1) * HD] = block[:, at : at + HD]
                kv[F + frame, rows_here, h * 2 * HD : (h + 1) * 2 * HD] = block[
                    :, at + HD : at + 3 * HD
                ]
            for side in (0, 1):
                halo_copy(side, u, way, chunk, frame).start()
        return carry

    lax.fori_loop(0, Z, gather_unit, 0)

    def halo_wait(u, carry):
        places = gather_place(u)
        for way in (0, 1):
            for side in (0, 1):
                halo_copy(side, u, way, *places[way]).wait_recv()
        return carry

    def spatial(chunk, frame):
        rows_here = pl.ds(pl.multiple_of(chunk * T, T), T)
        results = []
        for h in range(LH):
            queries = qb[frame, rows_here, h * HD : (h + 1) * HD]
            keys = kv[F + frame, :, h * 2 * HD : h * 2 * HD + HD]
            values = kv[F + frame, :, h * 2 * HD + HD : (h + 1) * 2 * HD]
            scores = lax.dot_general(queries, keys, NT, preferred_element_type=F32) * factor
            expo = jnp.exp(scores - jnp.max(scores, axis=1, keepdims=True))
            total = jnp.sum(expo, axis=1, keepdims=True)
            mixed = jnp.dot(expo.astype(BF16), values, preferred_element_type=F32)
            results.append(mixed / total)
        return results

    def temporal(chunk, frame):
        rows_here = pl.ds(pl.multiple_of(chunk * T, T), T)
        here = q * F + frame
        slot = slots[here]
        window = wins[here]
        gates = []
        for d in range(-WMAX, WMAX + 1):
            there = here + d
            inside = jnp.logical_and(there >= 0, there < FRAMES)
            gap = jnp.abs(slots[jnp.clip(there, 0, FRAMES - 1)] - slot)
            gates.append((jnp.logical_and(inside, gap <= window), gap.astype(F32) * NEAR_COST))
        results = []
        for h in range(LH):
            queries = qb[frame, rows_here, h * HD : (h + 1) * HD].astype(F32)
            logits = []
            for d in range(2 * WMAX + 1):
                keys = kv[F + frame + d - WMAX, rows_here, h * 2 * HD : h * 2 * HD + HD]
                score = jnp.sum(queries * keys.astype(F32), axis=1, keepdims=True) * factor
                allowed, cost = gates[d]
                logits.append(jnp.where(allowed, score - cost, -1e30))
            peak = functools.reduce(jnp.maximum, logits)
            total = jnp.zeros((T, 1), F32)
            mixed = jnp.zeros((T, HD), F32)
            for d in range(2 * WMAX + 1):
                weight = jnp.where(gates[d][0], jnp.exp(logits[d] - peak), 0.0)
                values = kv[
                    F + frame + d - WMAX, rows_here, h * 2 * HD + HD : (h + 1) * 2 * HD
                ]
                total = total + weight
                mixed = mixed + weight * values.astype(F32)
            results.append(mixed / total)
        return results

    def scatter_copy(way, n):
        src, dst = (sent_r, in_r) if way == 0 else (sent_l, in_l)
        return pltpu.make_async_remote_copy(
            src_ref=src.at[n - 1],
            dst_ref=dst.at[n + 1],
            send_sem=rs_send.at[way, n],
            recv_sem=rs_recv.at[way, n],
            device_id=(q, z_right if way == 0 else z_left),
            device_id_type=MESH,
        )

    def scatter_unit(n, carry):
        step = Z // 2 - n // 2
        right = (lax.rem(z + step, Z), lax.rem(n + 1, 2))
        left = (lax.rem(z + Z - step, Z), lax.rem(n, 2))
        spread = [spatial(*right), spatial(*left)]

        @pl.when(n == 1)
        def _():
            lax.fori_loop(0, Z, halo_wait, 0)

        along = [temporal(*right), temporal(*left)]
        for i in (0, 1):
            for h in range(LH):
                hd[i * T : (i + 1) * T, h * HD : (h + 1) * HD] = (
                    spread[i][h] + along[i][h]
                ).astype(BF16)

        @pl.when(n >= 3)
        def _():
            for way in (0, 1):
                scatter_copy(way, n - 2).wait_recv()

        tile = 512
        for c in range(0, D, tile):
            share = lax.dot_general(hd[...], wout[c : c + tile, :], NT, preferred_element_type=F32)
            sent_r[n - 1, :, c : c + tile] = (
                share[:T] + in_r[n - 1, :, c : c + tile].astype(F32)
            ).astype(BF16)
            sent_l[n - 1, :, c : c + tile] = (
                share[T:] + in_l[n - 1, :, c : c + tile].astype(F32)
            ).astype(BF16)

        @pl.when(n <= Z - 1)
        def _():
            for way in (0, 1):
                scatter_copy(way, n).start()

        return carry

    lax.fori_loop(1, Z + 1, scatter_unit, 0)

    fw_copy.wait()
    horizon = STRIDE * (FRAMES + 1)
    LAT = lat.shape[2]

    def schedule(f):
        ids = jnp.full((T, LAT), steps[f], jnp.int32)
        now = jnp.exp(ids.astype(F32) * (-DECAY / horizon))
        before = jnp.exp((ids - STRIDE).astype(F32) * (-DECAY / horizon))
        return jnp.sqrt(1.0 - now), jnp.sqrt(now), jnp.sqrt(before), jnp.sqrt(1.0 - before)

    tables = [schedule(f) for f in range(F)]
    for way in (0, 1):
        scatter_copy(way, Z - 1).wait_recv()
    edge = pltpu.make_async_remote_copy(
        src_ref=upd,
        dst_ref=got,
        send_sem=edge_send,
        recv_sem=edge_recv,
        device_id=(q_left, z),
        device_id_type=MESH,
    )
    for f, (mine, theirs) in enumerate(((sent_l, in_r), (sent_r, in_l))):
        total = mine[Z - 1].astype(F32) + theirs[Z].astype(F32)
        gate = mod[4 + f : 5 + f, :]
        block = (hid[f].astype(F32) + gate * total).astype(BF16)
        out[f] = block
        noise = lax.dot_general(block, fw[...], NT, preferred_element_type=F32)
        pred[f] = noise.astype(BF16)
        noise_now, root_now, root_before, noise_before = tables[f]
        clean = (lat[f].astype(F32) - noise_now * noise) / root_now
        updated = (root_before * clean + noise_before * noise).astype(BF16)
        if f == 0:
            upd[...] = updated
            edge.start()
        else:
            queue[f - 1] = updated
    edge.wait_recv()
    queue[F - 1] = jnp.where(q == Q - 1, fresh[...], got[...])

    edge.wait_send()
    for k in range(1, Z):
        mod_copy(k, z).wait_send()

    def drain(u, carry):
        places = gather_place(u)
        for way in (0, 1):
            chunk, frame = places[way]

            @pl.when(u >= 1)
            def _():
                gather_copy(way, u, xs.at[chunk, frame], chunk, frame).wait_send()
                scatter_copy(way, u).wait_send()

            for side in (0, 1):
                halo_copy(side, u, way, chunk, frame).wait_send()
        return carry

    lax.fori_loop(0, Z, drain, 0)


def shards(
    Q,
    Z,
    hidden,
    latent,
    fresh_noise,
    timesteps,
    queue_slots,
    windows,
    mod_weight,
    attention_weight,
    final_weight,
):
    T, F, D = hidden.shape
    LAT = latent.shape[2]
    W = attention_weight.shape[1]
    MP = mod_weight.shape[2]
    vmem = pl.BlockSpec(memory_space=pltpu.VMEM)
    smem = pl.BlockSpec(memory_space=pltpu.SMEM)
    hbm = pl.BlockSpec(memory_space=pl.ANY)
    dma = pltpu.SemaphoreType.DMA
    out, pred, queue = pl.pallas_call(
        functools.partial(kernel, Q, Z),
        out_shape=(
            jax.ShapeDtypeStruct((F, T, D), BF16),
            jax.ShapeDtypeStruct((F, T, LAT), BF16),
            jax.ShapeDtypeStruct((F, T, LAT), BF16),
        ),
        in_specs=[vmem, vmem, vmem, smem, smem, smem, hbm, hbm, hbm],
        out_specs=(vmem, vmem, vmem),
        scratch_shapes=[
            pltpu.VMEM((Z, F, T, D), BF16),
            pltpu.VMEM((D, W // 4 * 3), BF16),
            pltpu.VMEM((D, W // 4), BF16),
            pltpu.VMEM(mod_weight.shape, BF16),
            pltpu.VMEM((LAT, D), BF16),
            pltpu.VMEM((8, MP), F32),
            pltpu.VMEM((8, D), F32),
            pltpu.VMEM((2 * T, D), BF16),
            pltpu.VMEM((F, Z * T, W // 4), BF16),
            pltpu.VMEM((3 * F, Z * T, W // 2), BF16),
            pltpu.VMEM((2 * T, W // 4), BF16),
            pltpu.VMEM((Z, T, D), BF16),
            pltpu.VMEM((Z, T, D), BF16),
            pltpu.VMEM((Z + 1, T, D), BF16),
            pltpu.VMEM((Z + 1, T, D), BF16),
            pltpu.VMEM((T, LAT), BF16),
            pltpu.VMEM((T, LAT), BF16),
            dma((2 * (W // (4 * HD)),)),
            dma,
            dma,
            dma((Z,)),
            dma((Z,)),
            dma((2, Z)),
            dma((2, Z)),
            dma((2, 2, Z)),
            dma((2, 2, Z)),
            dma((2, Z)),
            dma((2, Z)),
            dma,
            dma,
        ],
        compiler_params=pltpu.CompilerParams(
            collective_id=0, has_side_effects=True, vmem_limit_bytes=56 * 1024 * 1024
        ),
        cost_estimate=pl.CostEstimate(
            flops=2 * Z * T * F * D * W, bytes_accessed=2 * D * W, transcendentals=0
        ),
    )(
        jnp.swapaxes(hidden, 0, 1),
        jnp.swapaxes(latent, 0, 1),
        fresh_noise,
        timesteps,
        queue_slots,
        windows,
        mod_weight,
        attention_weight,
        jnp.transpose(final_weight),
    )
    return jnp.swapaxes(out, 0, 1), jnp.swapaxes(pred, 0, 1), jnp.swapaxes(queue, 0, 1)


def solution(mesh):
    placed = (
        P("seq", "queue", None),
        P("seq", "queue", None),
        P("seq", None),
        P("queue"),
        P(),
        P(),
        P(None, None, "seq"),
        P(None, "seq"),
        P(),
    )
    return jax.shard_map(
        functools.partial(shards, mesh.shape["queue"], mesh.shape["seq"]),
        mesh=mesh,
        in_specs=placed,
        out_specs=(P("seq", "queue", None), P("seq", "queue", None), P("seq", "queue", None)),
        check_vma=False,
    )
```

```python
import functools
import math

import jax
import jax.numpy as jnp
from jax import lax
from jax.experimental import pallas as pl
from jax.experimental.pallas import tpu as pltpu
from jax.sharding import PartitionSpec as P

HD = 128
STRIDE = 16
WMAX = 2

LN_EPS = 1e-06
DECAY = 2.3
NEAR_COST = 0.5

MESH = pl.DeviceIdType.MESH
F32 = jnp.float32
BF16 = jnp.bfloat16
NT = (((1,), (1,)), ((), ()))


def kernel(
    Q,
    Z,
    hid_hbm,
    lat,
    fresh,
    steps,
    slots,
    wins,
    mw_hbm,
    w_hbm,
    fw_hbm,
    out,
    pred,
    queue,
    raw,
    xs,
    wqkv,
    wout,
    mw,
    fw,
    part,
    mod,
    norm,
    qb,
    kv,
    hd,
    share,
    sent_r,
    sent_l,
    in_r,
    in_l,
    upd,
    got,
    hid_sem,
    w_sem,
    mw_sem,
    fw_sem,
    mod_send,
    mod_recv,
    ag_send,
    ag_recv,
    halo_send,
    halo_recv,
    rs_send,
    rs_recv,
    edge_send,
    edge_recv,
):
    T, F, D = hid_hbm.shape
    LH = w_hbm.shape[1] // (4 * HD)
    MP = mw_hbm.shape[2]
    FREQ = mw_hbm.shape[1]
    FRAMES = F * Q
    factor = 1.0 / math.sqrt(HD)
    z = lax.axis_index("seq")
    q = lax.axis_index("queue")
    z_right, z_left = lax.rem(z + 1, Z), lax.rem(z + Z - 1, Z)
    q_right, q_left = lax.rem(q + 1, Q), lax.rem(q + Q - 1, Q)

    def weight_copies():
        copies = []
        for h in range(LH):
            copies.append(
                pltpu.make_async_copy(
                    w_hbm.at[:, pl.ds(h * 4 * HD, 3 * HD)],
                    wqkv.at[:, pl.ds(h * 3 * HD, 3 * HD)],
                    w_sem.at[h],
                )
            )
        for h in range(LH):
            copies.append(
                pltpu.make_async_copy(
                    w_hbm.at[:, pl.ds(h * 4 * HD + 3 * HD, HD)],
                    wout.at[:, pl.ds(h * HD, HD)],
                    w_sem.at[LH + h],
                )
            )
        return copies

    barrier = pltpu.get_barrier_semaphore()
    for k in range(1, Z):
        pl.semaphore_signal(
            barrier, inc=1, device_id=(q, lax.rem(z + k, Z)), device_id_type=MESH
        )
    for other in (q_left, q_right):
        pl.semaphore_signal(barrier, inc=1, device_id=(other, z), device_id_type=MESH)

    weights = weight_copies()
    hid_copy = pltpu.make_async_copy(hid_hbm, raw, hid_sem)
    mw_copy = pltpu.make_async_copy(mw_hbm, mw, mw_sem)
    fw_copy = pltpu.make_async_copy(fw_hbm, fw, fw_sem)
    hid_copy.start()
    mw_copy.start()
    for copy in weights:
        copy.start()
    fw_copy.start()

    def gather_copy(way, u, src, chunk, frame):
        return pltpu.make_async_remote_copy(
            src_ref=src,
            dst_ref=xs.at[chunk, frame],
            send_sem=ag_send.at[way, u],
            recv_sem=ag_recv.at[way, u],
            device_id=(q, z_right if way == 0 else z_left),
            device_id_type=MESH,
        )

    for slot in (0, 1):
        in_r[slot] = jnp.zeros((T, D), BF16)
        in_l[slot] = jnp.zeros((T, D), BF16)

    rows = lax.broadcasted_iota(jnp.int32, (8, FREQ), 0)
    lanes = lax.broadcasted_iota(jnp.int32, (8, FREQ), 1)
    half = FREQ // 2
    ladder = jnp.exp(lax.rem(lanes, half).astype(F32) * (-math.log(10000.0) / half))
    ids = jnp.where(lax.rem(rows, 2) == 0, steps[0], steps[1])
    angles = ids.astype(F32) * ladder
    freq = jnp.where(lanes < half, jnp.cos(angles), jnp.sin(angles))
    temb = (freq / (1.0 + jnp.exp(-freq))).astype(BF16)
    mw_copy.wait()
    rows = lax.broadcasted_iota(jnp.int32, (8, MP), 0)
    maps = [jnp.dot(temb, mw[p], preferred_element_type=F32) for p in range(3)]
    part[...] = jnp.where(rows < 2, maps[0], jnp.where(rows < 4, maps[1], maps[2]))

    def mod_copy(k, owner):
        return pltpu.make_async_remote_copy(
            src_ref=part,
            dst_ref=mod.at[:, pl.ds(pl.multiple_of(owner * MP, MP), MP)],
            send_sem=mod_send.at[k],
            recv_sem=mod_recv.at[k],
            device_id=(q, lax.rem(z + k, Z)),
            device_id_type=MESH,
        )

    hid_copy.wait()
    rows = lax.broadcasted_iota(jnp.int32, (F * T, F * T), 0)
    cols = lax.broadcasted_iota(jnp.int32, (F * T, F * T), 1)
    pick = (cols == F * lax.rem(rows, T) + lax.div(rows, T)).astype(BF16)
    by_frame = jnp.dot(pick, raw[...].reshape(F * T, D), preferred_element_type=F32).astype(BF16)
    for f in range(F):
        xs[z, f] = by_frame[f * T : (f + 1) * T]

    pl.semaphore_wait(barrier, Z + 1)
    for k in range(1, Z):
        mod_copy(k, z).start()
    for u in (1, 2):
        gather_copy(0, u, xs.at[z, u - 1], z, u - 1).start()
        gather_copy(1, u, xs.at[z, 2 - u], z, 2 - u).start()
    mod[:, pl.ds(pl.multiple_of(z * MP, MP), MP)] = part[...]

    def normalise(chunk, frame, base):
        scale = 1.0 + mod[pl.ds(2 + frame, 1), :]
        shift = mod[pl.ds(frame, 1), :]
        for r in range(0, T, 16):
            x = xs[chunk, frame, r : r + 16, :].astype(F32)
            centred = x - jnp.sum(x, axis=1, keepdims=True) * (1.0 / D)
            variance = jnp.sum(centred * centred, axis=1, keepdims=True) * (1.0 / D)
            y = centred * lax.rsqrt(variance + LN_EPS) * scale + shift
            norm[base + r : base + r + 16, :] = y.astype(BF16)

    def halo_copy(side, u, i, chunk, frame):
        rows_here = pl.ds(pl.multiple_of(chunk * T, T), T)
        return pltpu.make_async_remote_copy(
            src_ref=kv.at[F + frame, rows_here],
            dst_ref=kv.at[frame + (0 if side == 0 else 2 * F), rows_here],
            send_sem=halo_send.at[side, i, u],
            recv_sem=halo_recv.at[side, i, u],
            device_id=(q_right if side == 0 else q_left, z),
            device_id_type=MESH,
        )

    def gather_place(u):
        step = (u + 1) // 2
        left = (lax.rem(z + Z - step, Z), lax.rem(u + 1, 2))
        right = (lax.rem(z + step, Z), lax.rem(u, 2))
        return left, right

    def pass_on(u):
        places = gather_place(u)
        for way in (0, 1):
            chunk, frame = places[way]
            gather_copy(way, u, xs.at[chunk, frame], chunk, frame).wait_recv()

            @pl.when(u + 2 <= Z - 1)
            def _():
                gather_copy(way, u + 2, xs.at[chunk, frame], chunk, frame).start()

    pass_on(1)
    for k in range(1, Z):
        mod_copy(k, lax.rem(z + Z - k, Z)).wait_recv()
    for copy in weights:
        copy.wait()

    def gather_unit(u, carry):
        places = gather_place(u)
        pl.when(u >= 2)(lambda: pass_on(u))

        for way in (0, 1):
            normalise(*places[way], way * T)
        projected = jnp.dot(norm[...], wqkv[...], preferred_element_type=F32).astype(BF16)
        for way in (0, 1):
            chunk, frame = places[way]
            rows_here = pl.ds(pl.multiple_of(chunk * T, T), T)
            block = projected[way * T : (way + 1) * T]
            for h in range(LH):
                at = h * 3 * HD
                qb[frame, rows_here, h * HD : (h + 1) * HD] = block[:, at : at + HD]
                kv[F + frame, rows_here, h * 2 * HD : (h + 1) * 2 * HD] = block[
                    :, at + HD : at + 3 * HD
                ]
            for side in (0, 1):
                halo_copy(side, u, way, chunk, frame).start()
        return carry

    lax.fori_loop(0, Z, gather_unit, 0)

    def halo_wait(u, carry):
        places = gather_place(u)
        for way in (0, 1):
            for side in (0, 1):
                halo_copy(side, u, way, *places[way]).wait_recv()
        return carry

    def spatial(chunk, frame):
        rows_here = pl.ds(pl.multiple_of(chunk * T, T), T)
        results = []
        for h in range(LH):
            queries = qb[frame, rows_here, h * HD : (h + 1) * HD]
            keys = kv[F + frame, :, h * 2 * HD : h * 2 * HD + HD]
            values = kv[F + frame, :, h * 2 * HD + HD : (h + 1) * 2 * HD]
            scores = lax.dot_general(queries, keys, NT, preferred_element_type=F32) * factor
            expo = jnp.exp(scores - jnp.max(scores, axis=1, keepdims=True))
            total = jnp.sum(expo, axis=1, keepdims=True)
            mixed = jnp.dot(expo.astype(BF16), values, preferred_element_type=F32)
            results.append(mixed / total)
        return results

    def temporal(chunk, frame):
        rows_here = pl.ds(pl.multiple_of(chunk * T, T), T)
        here = q * F + frame
        slot = slots[here]
        window = wins[here]
        gates = []
        for d in range(-WMAX, WMAX + 1):
            there = here + d
            inside = jnp.logical_and(there >= 0, there < FRAMES)
            gap = jnp.abs(slots[jnp.clip(there, 0, FRAMES - 1)] - slot)
            gates.append((jnp.logical_and(inside, gap <= window), gap.astype(F32) * NEAR_COST))
        results = []
        for h in range(LH):
            queries = qb[frame, rows_here, h * HD : (h + 1) * HD].astype(F32)
            logits = []
            for d in range(2 * WMAX + 1):
                keys = kv[F + frame + d - WMAX, rows_here, h * 2 * HD : h * 2 * HD + HD]
                score = jnp.sum(queries * keys.astype(F32), axis=1, keepdims=True) * factor
                allowed, cost = gates[d]
                logits.append(jnp.where(allowed, score - cost, -1e30))
            peak = functools.reduce(jnp.maximum, logits)
            total = jnp.zeros((T, 1), F32)
            mixed = jnp.zeros((T, HD), F32)
            for d in range(2 * WMAX + 1):
                weight = jnp.where(gates[d][0], jnp.exp(logits[d] - peak), 0.0)
                values = kv[
                    F + frame + d - WMAX, rows_here, h * 2 * HD + HD : (h + 1) * 2 * HD
                ]
                total = total + weight
                mixed = mixed + weight * values.astype(F32)
            results.append(mixed / total)
        return results

    half = T // 2

    def scatter_copy(way, n, part_of):
        src, dst = (sent_r, in_r) if way == 0 else (sent_l, in_l)
        rows_here = pl.ds(part_of * half, half)
        return pltpu.make_async_remote_copy(
            src_ref=src.at[n - 1, rows_here],
            dst_ref=dst.at[n + 1, rows_here],
            send_sem=rs_send.at[way, part_of, n],
            recv_sem=rs_recv.at[way, part_of, n],
            device_id=(q, z_right if way == 0 else z_left),
            device_id_type=MESH,
        )

    def scatter_unit(n, carry):
        step = Z // 2 - n // 2
        late = n // (Z - 2) - n // Z
        right = (lax.rem(z + step, Z), lax.rem(n + 1 + late, 2))
        left = (lax.rem(z + Z - step, Z), lax.rem(n, 2))
        spread = [spatial(*right), spatial(*left)]

        @pl.when(n == 1)
        def _():
            lax.fori_loop(0, Z, halo_wait, 0)

        along = [temporal(*right), temporal(*left)]
        for i in (0, 1):
            for h in range(LH):
                hd[i * T : (i + 1) * T, h * HD : (h + 1) * HD] = (
                    spread[i][h] + along[i][h]
                ).astype(BF16)
        tile = 512
        for c in range(0, D, tile):
            share[:, c : c + tile] = lax.dot_general(
                hd[...], wout[c : c + tile, :], NT, preferred_element_type=F32
            )

        @pl.when(n <= Z - 1)
        def _():
            needs = (n - 2 + late * (2 * Z - 3 - 2 * n), n - 2)
            for part_of in (0, 1):
                for way, (sent, arrived) in enumerate(((sent_r, in_r), (sent_l, in_l))):
                    need = needs[way]

                    @pl.when(n >= 3)
                    def _():
                        scatter_copy(way, need, part_of).wait_recv()

                    mine = way * T + part_of * half
                    rows_here = slice(part_of * half, (part_of + 1) * half)
                    sent[n - 1, rows_here, :] = (
                        share[mine : mine + half, :] + arrived[need + 1, rows_here, :].astype(F32)
                    ).astype(BF16)
                    scatter_copy(way, n, part_of).start()

        return carry

    lax.fori_loop(1, Z + 1, scatter_unit, 0)

    fw_copy.wait()
    horizon = STRIDE * (FRAMES + 1)
    LAT = lat.shape[2]

    def schedule(f):
        ids = jnp.full((T, LAT), steps[f], jnp.int32)
        now = jnp.exp(ids.astype(F32) * (-DECAY / horizon))
        before = jnp.exp((ids - STRIDE).astype(F32) * (-DECAY / horizon))
        return jnp.sqrt(1.0 - now), jnp.sqrt(now), jnp.sqrt(before), jnp.sqrt(1.0 - before)

    tables = [schedule(f) for f in range(F)]
    edge = pltpu.make_async_remote_copy(
        src_ref=upd,
        dst_ref=got,
        send_sem=edge_send,
        recv_sem=edge_recv,
        device_id=(q_left, z),
        device_id_type=MESH,
    )
    for f in range(F):
        for way in (0, 1):
            for part_of in (0, 1):
                scatter_copy(way, Z - 2 + f, part_of).wait_recv()
        mine = (1 - f) * T
        total = (
            share[mine : mine + T, :]
            + in_r[Z - 1 + f].astype(F32)
            + in_l[Z - 1 + f].astype(F32)
        )
        gate = mod[4 + f : 5 + f, :]
        block = (xs[z, f].astype(F32) + gate * total).astype(BF16)
        out[f] = block
        noise = lax.dot_general(block, fw[...], NT, preferred_element_type=F32)
        pred[f] = noise.astype(BF16)
        noise_now, root_now, root_before, noise_before = tables[f]
        clean = (lat[:, f, :].astype(F32) - noise_now * noise) / root_now
        updated = (root_before * clean + noise_before * noise).astype(BF16)
        if f == 0:
            upd[...] = updated
            edge.start()
        else:
            queue[f - 1] = updated
    edge.wait_recv()
    queue[F - 1] = jnp.where(q == Q - 1, fresh[...], got[...])

    edge.wait_send()
    for k in range(1, Z):
        mod_copy(k, z).wait_send()

    def drain(u, carry):
        places = gather_place(u)
        for way in (0, 1):
            chunk, frame = places[way]

            @pl.when(u >= 1)
            def _():
                gather_copy(way, u, xs.at[chunk, frame], chunk, frame).wait_send()
                for part_of in (0, 1):
                    scatter_copy(way, u, part_of).wait_send()

            for side in (0, 1):
                halo_copy(side, u, way, chunk, frame).wait_send()
        return carry

    lax.fori_loop(0, Z, drain, 0)


def by_token(*refs):
    for src, dst in zip(refs[:3], refs[3:]):
        for f in range(src.shape[0]):
            dst[:, f, :] = src[f]


def shards(
    Q,
    Z,
    hidden,
    latent,
    fresh_noise,
    timesteps,
    queue_slots,
    windows,
    mod_weight,
    attention_weight,
    final_weight,
):
    T, F, D = hidden.shape
    LAT = latent.shape[2]
    W = attention_weight.shape[1]
    MP = mod_weight.shape[2]
    vmem = pl.BlockSpec(memory_space=pltpu.VMEM)
    smem = pl.BlockSpec(memory_space=pltpu.SMEM)
    hbm = pl.BlockSpec(memory_space=pltpu.HBM)
    dma = pltpu.SemaphoreType.DMA
    out, pred, queue = pl.pallas_call(
        functools.partial(kernel, Q, Z),
        out_shape=(
            jax.ShapeDtypeStruct((F, T, D), BF16),
            jax.ShapeDtypeStruct((F, T, LAT), BF16),
            jax.ShapeDtypeStruct((F, T, LAT), BF16),
        ),
        in_specs=[hbm, vmem, vmem, smem, smem, smem, hbm, hbm, hbm],
        out_specs=(vmem, vmem, vmem),
        scratch_shapes=[
            pltpu.VMEM((T, F, D), BF16),
            pltpu.VMEM((Z, F, T, D), BF16),
            pltpu.VMEM((D, W // 4 * 3), BF16),
            pltpu.VMEM((D, W // 4), BF16),
            pltpu.VMEM(mod_weight.shape, BF16),
            pltpu.VMEM((LAT, D), BF16),
            pltpu.VMEM((8, MP), F32),
            pltpu.VMEM((8, D), F32),
            pltpu.VMEM((2 * T, D), BF16),
            pltpu.VMEM((F, Z * T, W // 4), BF16),
            pltpu.VMEM((3 * F, Z * T, W // 2), BF16),
            pltpu.VMEM((2 * T, W // 4), BF16),
            pltpu.VMEM((2 * T, D), F32),
            pltpu.VMEM((Z - 1, T, D), BF16),
            pltpu.VMEM((Z - 1, T, D), BF16),
            pltpu.VMEM((Z + 1, T, D), BF16),
            pltpu.VMEM((Z + 1, T, D), BF16),
            pltpu.VMEM((T, LAT), BF16),
            pltpu.VMEM((T, LAT), BF16),
            dma,
            dma((2 * (W // (4 * HD)),)),
            dma,
            dma,
            dma((Z,)),
            dma((Z,)),
            dma((2, Z)),
            dma((2, Z)),
            dma((2, 2, Z)),
            dma((2, 2, Z)),
            dma((2, 2, Z)),
            dma((2, 2, Z)),
            dma,
            dma,
        ],
        compiler_params=pltpu.CompilerParams(
            collective_id=0, has_side_effects=True, vmem_limit_bytes=56 * 1024 * 1024
        ),
        cost_estimate=pl.CostEstimate(
            flops=2 * Z * T * F * D * W, bytes_accessed=2 * D * W, transcendentals=0
        ),
    )(
        hidden,
        latent,
        fresh_noise,
        timesteps,
        queue_slots,
        windows,
        mod_weight,
        attention_weight,
        jnp.transpose(final_weight),
    )
    return pl.pallas_call(
        by_token,
        out_shape=tuple(
            jax.ShapeDtypeStruct((T, F, x.shape[2]), BF16) for x in (out, pred, queue)
        ),
        in_specs=[vmem] * 3,
        out_specs=(vmem,) * 3,
    )(out, pred, queue)


def solution(mesh):
    placed = (
        P("seq", "queue", None),
        P("seq", "queue", None),
        P("seq", None),
        P("queue"),
        P(),
        P(),
        P(None, None, "seq"),
        P(None, "seq"),
        P(),
    )
    return jax.shard_map(
        functools.partial(shards, mesh.shape["queue"], mesh.shape["seq"]),
        mesh=mesh,
        in_specs=placed,
        out_specs=(P("seq", "queue", None), P("seq", "queue", None), P("seq", "queue", None)),
        check_vma=False,
    )
```

```python
import functools
import math

import jax
import jax.numpy as jnp
from jax import lax
from jax.experimental import pallas as pl
from jax.experimental.pallas import tpu as pltpu
from jax.sharding import PartitionSpec as P

HD = 128
STRIDE = 16
WMAX = 2

LN_EPS = 1e-06
DECAY = 2.3
NEAR_COST = 0.5

MESH = pl.DeviceIdType.MESH
F32 = jnp.float32
BF16 = jnp.bfloat16
NT = (((1,), (1,)), ((), ()))


def table(n, values):
    result = values[0]
    for k in range(1, len(values)):
        if values[k] != values[k - 1]:
            result = result + (values[k] - values[k - 1]) * ((n + len(values) - k) // len(values))
    return result


def kernel(
    Q,
    Z,
    hid_hbm,
    lat_hbm,
    fresh_hbm,
    steps_hbm,
    slots_hbm,
    wins_hbm,
    mw_hbm,
    w_hbm,
    fw_hbm,
    out,
    pred,
    queue,
    lat,
    fresh,
    steps,
    slots,
    wins,
    xs,
    own,
    wqkv,
    wout,
    mw,
    fw,
    part,
    mod,
    pattern,
    norm,
    qb,
    kv,
    hd,
    share,
    sent_r,
    sent_l,
    in_r,
    in_l,
    upd,
    got,
    small_sem,
    w_sem,
    mw_sem,
    fw_sem,
    mod_send,
    mod_recv,
    ag_send,
    ag_recv,
    halo_send,
    halo_recv,
    rs_send,
    rs_recv,
    edge_send,
    edge_recv,
):
    T, F, D = hid_hbm.shape
    LH = w_hbm.shape[1] // (4 * HD)
    MP = mw_hbm.shape[2]
    FREQ = mw_hbm.shape[1]
    FRAMES = F * Q
    factor = 1.0 / math.sqrt(HD)
    z = lax.axis_index("seq")
    q = lax.axis_index("queue")
    z_right, z_left = lax.rem(z + 1, Z), lax.rem(z + Z - 1, Z)
    q_right, q_left = lax.rem(q + 1, Q), lax.rem(q + Q - 1, Q)

    def weight_copies():
        copies = []
        for h in range(LH):
            copies.append(
                pltpu.make_async_copy(
                    w_hbm.at[:, pl.ds(h * 4 * HD, 3 * HD)],
                    wqkv.at[:, pl.ds(h * 3 * HD, 3 * HD)],
                    w_sem.at[h],
                )
            )
        for h in range(LH):
            copies.append(
                pltpu.make_async_copy(
                    w_hbm.at[:, pl.ds(h * 4 * HD + 3 * HD, HD)],
                    wout.at[:, pl.ds(h * HD, HD)],
                    w_sem.at[LH + h],
                )
            )
        return copies

    barrier = pltpu.get_barrier_semaphore()
    for k in range(1, Z):
        pl.semaphore_signal(
            barrier, inc=1, device_id=(q, lax.rem(z + k, Z)), device_id_type=MESH
        )
    for other in (q_left, q_right):
        pl.semaphore_signal(barrier, inc=1, device_id=(other, z), device_id_type=MESH)

    weights = weight_copies()
    small = [
        pltpu.make_async_copy(src, dst, small_sem.at[i])
        for i, (src, dst) in enumerate(
            (
                (steps_hbm, steps),
                (slots_hbm, slots),
                (wins_hbm, wins),
                (lat_hbm, lat),
                (fresh_hbm, fresh),
                (hid_hbm, xs.at[z]),
            )
        )
    ]
    mw_copy = pltpu.make_async_copy(mw_hbm, mw, mw_sem)
    fw_copy = pltpu.make_async_copy(fw_hbm, fw, fw_sem)
    small[0].start()
    mw_copy.start()
    half = T // 2

    def piece(chunk, part_of):
        return xs.at[chunk, pl.ds(part_of * half, half)]

    def gather_copy(way, u, src, chunk, part_of):
        return pltpu.make_async_remote_copy(
            src_ref=src,
            dst_ref=piece(chunk, part_of),
            send_sem=ag_send.at[way, u],
            recv_sem=ag_recv.at[way, u],
            device_id=(q, z_right if way == 0 else z_left),
            device_id_type=MESH,
        )

    def own_copies(u):
        for way in (0, 1):
            part_of = u - 1 if way == 0 else 2 - u
            gather_copy(way, u, hid_hbm.at[pl.ds(part_of * half, half)], z, part_of).start()

    pl.semaphore_wait(barrier, Z + 1)
    own_copies(1)

    small[0].wait()
    rows = lax.broadcasted_iota(jnp.int32, (8, FREQ), 0)
    lanes = lax.broadcasted_iota(jnp.int32, (8, FREQ), 1)
    waves = FREQ // 2
    ladder = jnp.exp(lax.rem(lanes, waves).astype(F32) * (-math.log(10000.0) / waves))
    ids = jnp.where(lax.rem(rows, 2) == 0, steps[0], steps[1])
    angles = ids.astype(F32) * ladder
    freq = jnp.where(lanes < waves, jnp.cos(angles), jnp.sin(angles))
    temb = (freq / (1.0 + jnp.exp(-freq))).astype(BF16)
    mw_copy.wait()
    rows = lax.broadcasted_iota(jnp.int32, (8, MP), 0)
    maps = [jnp.dot(temb, mw[p], preferred_element_type=F32) for p in range(3)]
    part[...] = jnp.where(rows < 2, maps[0], jnp.where(rows < 4, maps[1], maps[2]))

    def mod_copy(k, owner):
        return pltpu.make_async_remote_copy(
            src_ref=part,
            dst_ref=mod.at[:, pl.ds(pl.multiple_of(owner * MP, MP), MP)],
            send_sem=mod_send.at[k],
            recv_sem=mod_recv.at[k],
            device_id=(q, lax.rem(z + k, Z)),
            device_id_type=MESH,
        )

    for k in range(1, Z):
        mod_copy(k, z).start()
    own_copies(2)
    for copy in small[1:] + weights + [fw_copy]:
        copy.start()
    mod[:, pl.ds(pl.multiple_of(z * MP, MP), MP)] = part[...]
    in_r[0] = jnp.zeros((T, D), BF16)
    in_l[0] = jnp.zeros((T, D), BF16)

    def choice(rows_count, column_of):
        rows = lax.broadcasted_iota(jnp.int32, (rows_count, rows_count), 0)
        cols = lax.broadcasted_iota(jnp.int32, (rows_count, rows_count), 1)
        return (cols == column_of(rows)).astype(BF16)

    for copy in small[1:]:
        copy.wait()
    by_frame = choice(F * T, lambda r: F * lax.rem(r, T) + lax.div(r, T))
    own_rows = jnp.dot(by_frame, xs[z].reshape(F * T, D), preferred_element_type=F32).astype(BF16)
    for f in range(F):
        own[f] = own_rows[f * T : (f + 1) * T]

    def pass_on(u):
        places = gather_place(u)
        for way in (0, 1):
            chunk, part_of = places[way]
            gather_copy(way, u, piece(chunk, part_of), chunk, part_of).wait_recv()

            @pl.when(u + 2 <= Z - 1)
            def _():
                gather_copy(way, u + 2, piece(chunk, part_of), chunk, part_of).start()

    def gather_place(u):
        step = (u + 1) // 2
        left = (lax.rem(z + Z - step, Z), lax.rem(u + 1, 2))
        right = (lax.rem(z + step, Z), lax.rem(u, 2))
        return left, right

    pass_on(1)
    for k in range(1, Z):
        mod_copy(k, lax.rem(z + Z - k, Z)).wait_recv()
    rows = lax.broadcasted_iota(jnp.int32, (8, D), 0)
    for p in (0, 1):
        pattern[p] = jnp.where(
            lax.rem(rows, 2) == 0, mod[2 * p : 2 * p + 1, :], mod[2 * p + 1 : 2 * p + 2, :]
        ) + float(p)
    for copy in weights:
        copy.wait()

    def normalise(chunk, part_of, base):
        for r in range(0, half, 8):
            x = xs[chunk, pl.ds(part_of * half + r, 8)].reshape(16, D).astype(F32)
            centred = x - jnp.sum(x, axis=1, keepdims=True) * (1.0 / D)
            variance = jnp.sum(centred * centred, axis=1, keepdims=True) * (1.0 / D)
            y = (centred * lax.rsqrt(variance + LN_EPS)).reshape(2, 8, D)
            y = y * pattern[1][None] + pattern[0][None]
            norm[base + F * r : base + F * r + 16, :] = y.reshape(16, D).astype(BF16)

    def token_rows(chunk, part_of):
        return pl.ds(pl.multiple_of(chunk * T + part_of * half, half), half)

    def halo_copy(side, u, i, chunk, part_of):
        rows_here = token_rows(chunk, part_of)
        return pltpu.make_async_remote_copy(
            src_ref=kv.at[pl.ds(F, F), rows_here],
            dst_ref=kv.at[pl.ds(0 if side == 0 else 2 * F, F), rows_here],
            send_sem=halo_send.at[side, i, u],
            recv_sem=halo_recv.at[side, i, u],
            device_id=(q_right if side == 0 else q_left, z),
            device_id_type=MESH,
        )

    split = choice(
        2 * T,
        lambda r: lax.rem(lax.div(r, half), 2) * T + F * lax.rem(r, half) + lax.div(r, T),
    )

    def gather_unit(u, carry):
        places = gather_place(u)
        pl.when(u >= 2)(lambda: pass_on(u))

        for way in (0, 1):
            normalise(*places[way], way * T)
        mixed_rows = jnp.dot(norm[...], wqkv[...], preferred_element_type=F32).astype(BF16)
        projected = jnp.dot(split, mixed_rows, preferred_element_type=F32).astype(BF16)
        for way in (0, 1):
            rows_here = token_rows(*places[way])
            for f in range(F):
                at_row = f * T + way * half
                block = projected[at_row : at_row + half]
                for h in range(LH):
                    at = h * 3 * HD
                    qb[f, rows_here, h * HD : (h + 1) * HD] = block[:, at : at + HD]
                    kv[F + f, rows_here, h * 2 * HD : (h + 1) * 2 * HD] = block[
                        :, at + HD : at + 3 * HD
                    ]
            for side in (0, 1):
                halo_copy(side, u, way, *places[way]).start()
        return carry

    lax.fori_loop(0, Z, gather_unit, 0)

    def halo_wait(u, carry):
        places = gather_place(u)
        for way in (0, 1):
            for side in (0, 1):
                halo_copy(side, u, way, *places[way]).wait_recv()
        return carry

    def spatial(chunk, frame):
        rows_here = pl.ds(pl.multiple_of(chunk * T, T), T)
        results = []
        for h in range(LH):
            queries = qb[frame, rows_here, h * HD : (h + 1) * HD]
            keys = kv[F + frame, :, h * 2 * HD : h * 2 * HD + HD]
            values = kv[F + frame, :, h * 2 * HD + HD : (h + 1) * 2 * HD]
            scores = lax.dot_general(queries, keys, NT, preferred_element_type=F32) * factor
            expo = jnp.exp(scores - jnp.max(scores, axis=1, keepdims=True))
            total = jnp.sum(expo, axis=1, keepdims=True)
            mixed = jnp.dot(expo.astype(BF16), values, preferred_element_type=F32)
            results.append(mixed / total)
        return results

    def temporal(chunk, frame):
        rows_here = pl.ds(pl.multiple_of(chunk * T, T), T)
        here = q * F + frame
        slot = slots[here]
        window = wins[here]
        gates = []
        for d in range(-WMAX, WMAX + 1):
            there = here + d
            inside = jnp.logical_and(there >= 0, there < FRAMES)
            gap = jnp.abs(slots[jnp.clip(there, 0, FRAMES - 1)] - slot)
            gates.append((jnp.logical_and(inside, gap <= window), gap.astype(F32) * NEAR_COST))
        results = []
        for h in range(LH):
            queries = qb[frame, rows_here, h * HD : (h + 1) * HD].astype(F32)
            logits = []
            for d in range(2 * WMAX + 1):
                keys = kv[F + frame + d - WMAX, rows_here, h * 2 * HD : h * 2 * HD + HD]
                score = jnp.sum(queries * keys.astype(F32), axis=1, keepdims=True) * factor
                allowed, cost = gates[d]
                logits.append(jnp.where(allowed, score - cost, -1e30))
            peak = functools.reduce(jnp.maximum, logits)
            total = jnp.zeros((T, 1), F32)
            mixed = jnp.zeros((T, HD), F32)
            for d in range(2 * WMAX + 1):
                weight = jnp.where(gates[d][0], jnp.exp(logits[d] - peak), 0.0)
                values = kv[
                    F + frame + d - WMAX, rows_here, h * 2 * HD + HD : (h + 1) * 2 * HD
                ]
                total = total + weight
                mixed = mixed + weight * values.astype(F32)
            results.append(mixed / total)
        return results

    def scatter_copy(way, n, part_of):
        src, dst = (sent_r, in_r) if way == 0 else (sent_l, in_l)
        rows_here = pl.ds(part_of * half, half)
        return pltpu.make_async_remote_copy(
            src_ref=src.at[n - 1, rows_here],
            dst_ref=dst.at[n, rows_here],
            send_sem=rs_send.at[way, part_of, n],
            recv_sem=rs_recv.at[way, part_of, n],
            device_id=(q, z_right if way == 0 else z_left),
            device_id_type=MESH,
        )

    def scatter_unit(n, carry):
        right_step = table(n, (0, 3, 4, 2, 3, 2, 1, 1, 0))
        left_step = table(n, (0, 3, 4, 2, 3, 1, 2, 1, 0))
        right = (lax.rem(z + right_step, Z), table(n, (1, 1, 0, 1, 0, 0, 0, 1, 1)))
        left = (lax.rem(z + Z - left_step, Z), table(n, (0, 0, 1, 0, 1, 0, 1, 1, 0)))
        spread = [spatial(*right), spatial(*left)]

        @pl.when(n == 1)
        def _():
            lax.fori_loop(0, Z - 1, halo_wait, 0)

        @pl.when(n == 2)
        def _():
            halo_wait(Z - 1, 0)

        along = [temporal(*right), temporal(*left)]
        for i in (0, 1):
            for h in range(LH):
                hd[i * T : (i + 1) * T, h * HD : (h + 1) * HD] = (
                    spread[i][h] + along[i][h]
                ).astype(BF16)
        tile = 512
        for c in range(0, D, tile):
            share[:, c : c + tile] = lax.dot_general(
                hd[...], wout[c : c + tile, :], NT, preferred_element_type=F32
            )

        @pl.when(n <= Z - 1)
        def _():
            needs = (
                table(n, (0, 0, 0, 1, 2, 4, 5, 3, 0)),
                table(n, (0, 0, 0, 1, 2, 3, 4, 6, 0)),
            )
            for part_of in (0, 1):
                for way, (sent, arrived) in enumerate(((sent_r, in_r), (sent_l, in_l))):
                    need = needs[way]

                    @pl.when(n >= 3)
                    def _():
                        scatter_copy(way, need, part_of).wait_recv()

                    mine = way * T + part_of * half
                    rows_here = slice(part_of * half, (part_of + 1) * half)
                    sent[n - 1, rows_here, :] = (
                        share[mine : mine + half, :] + arrived[need, rows_here, :].astype(F32)
                    ).astype(BF16)
                    scatter_copy(way, n, part_of).start()

        return carry

    lax.fori_loop(1, Z + 1, scatter_unit, 0)

    fw_copy.wait()
    horizon = STRIDE * (FRAMES + 1)
    LAT = lat.shape[2]

    def schedule(f):
        ids = jnp.full((T, LAT), steps[f], jnp.int32)
        now = jnp.exp(ids.astype(F32) * (-DECAY / horizon))
        before = jnp.exp((ids - STRIDE).astype(F32) * (-DECAY / horizon))
        return jnp.sqrt(1.0 - now), jnp.sqrt(now), jnp.sqrt(before), jnp.sqrt(1.0 - before)

    tables = [schedule(f) for f in range(F)]
    edge = pltpu.make_async_remote_copy(
        src_ref=upd,
        dst_ref=got,
        send_sem=edge_send,
        recv_sem=edge_recv,
        device_id=(q_left, z),
        device_id_type=MESH,
    )
    last = ((6, 5), (7, 7))
    for f in range(F):
        for way in (0, 1):
            for part_of in (0, 1):
                scatter_copy(way, last[f][way], part_of).wait_recv()
        mine = (1 - f) * T
        total = (
            share[mine : mine + T, :]
            + in_r[last[f][0]].astype(F32)
            + in_l[last[f][1]].astype(F32)
        )
        gate = mod[4 + f : 5 + f, :]
        block = (own[f].astype(F32) + gate * total).astype(BF16)
        out[f] = block
        noise = lax.dot_general(block, fw[...], NT, preferred_element_type=F32)
        pred[f] = noise.astype(BF16)
        noise_now, root_now, root_before, noise_before = tables[f]
        clean = (lat[:, f, :].astype(F32) - noise_now * noise) / root_now
        updated = (root_before * clean + noise_before * noise).astype(BF16)
        if f == 0:
            upd[...] = updated
            edge.start()
        else:
            queue[f - 1] = updated
    edge.wait_recv()
    queue[F - 1] = jnp.where(q == Q - 1, fresh[...], got[...])

    edge.wait_send()
    for k in range(1, Z):
        mod_copy(k, z).wait_send()

    def drain(u, carry):
        places = gather_place(u)
        for way in (0, 1):
            chunk, part_of = places[way]

            @pl.when(u >= 1)
            def _():
                gather_copy(way, u, piece(chunk, part_of), chunk, part_of).wait_send()
                for rows_part in (0, 1):
                    scatter_copy(way, u, rows_part).wait_send()

            for side in (0, 1):
                halo_copy(side, u, way, chunk, part_of).wait_send()
        return carry

    lax.fori_loop(0, Z, drain, 0)


def by_token(*refs):
    for src, dst in zip(refs[:3], refs[3:]):
        for f in range(src.shape[0]):
            dst[:, f, :] = src[f]


def shards(
    Q,
    Z,
    hidden,
    latent,
    fresh_noise,
    timesteps,
    queue_slots,
    windows,
    mod_weight,
    attention_weight,
    final_weight,
):
    T, F, D = hidden.shape
    LAT = latent.shape[2]
    W = attention_weight.shape[1]
    MP = mod_weight.shape[2]
    vmem = pl.BlockSpec(memory_space=pltpu.VMEM)
    hbm = pl.BlockSpec(memory_space=pltpu.HBM)
    dma = pltpu.SemaphoreType.DMA
    out, pred, queue = pl.pallas_call(
        functools.partial(kernel, Q, Z),
        out_shape=(
            jax.ShapeDtypeStruct((F, T, D), BF16),
            jax.ShapeDtypeStruct((F, T, LAT), BF16),
            jax.ShapeDtypeStruct((F, T, LAT), BF16),
        ),
        in_specs=[hbm] * 9,
        out_specs=(vmem, vmem, vmem),
        scratch_shapes=[
            pltpu.VMEM(latent.shape, BF16),
            pltpu.VMEM(fresh_noise.shape, BF16),
            pltpu.SMEM(timesteps.shape, jnp.int32),
            pltpu.SMEM(queue_slots.shape, jnp.int32),
            pltpu.SMEM(windows.shape, jnp.int32),
            pltpu.VMEM((Z, T, F, D), BF16),
            pltpu.VMEM((F, T, D), BF16),
            pltpu.VMEM((D, W // 4 * 3), BF16),
            pltpu.VMEM((D, W // 4), BF16),
            pltpu.VMEM(mod_weight.shape, BF16),
            pltpu.VMEM((LAT, D), BF16),
            pltpu.VMEM((8, MP), F32),
            pltpu.VMEM((8, D), F32),
            pltpu.VMEM((2, 8, D), F32),
            pltpu.VMEM((2 * T, D), BF16),
            pltpu.VMEM((F, Z * T, W // 4), BF16),
            pltpu.VMEM((3 * F, Z * T, W // 2), BF16),
            pltpu.VMEM((2 * T, W // 4), BF16),
            pltpu.VMEM((2 * T, D), F32),
            pltpu.VMEM((Z - 1, T, D), BF16),
            pltpu.VMEM((Z - 1, T, D), BF16),
            pltpu.VMEM((Z, T, D), BF16),
            pltpu.VMEM((Z, T, D), BF16),
            pltpu.VMEM((T, LAT), BF16),
            pltpu.VMEM((T, LAT), BF16),
            dma((6,)),
            dma((2 * (W // (4 * HD)),)),
            dma,
            dma,
            dma((Z,)),
            dma((Z,)),
            dma((2, Z)),
            dma((2, Z)),
            dma((2, 2, Z)),
            dma((2, 2, Z)),
            dma((2, 2, Z)),
            dma((2, 2, Z)),
            dma,
            dma,
        ],
        compiler_params=pltpu.CompilerParams(
            collective_id=0, has_side_effects=True, vmem_limit_bytes=56 * 1024 * 1024
        ),
        cost_estimate=pl.CostEstimate(
            flops=2 * Z * T * F * D * W, bytes_accessed=2 * D * W, transcendentals=0
        ),
    )(
        hidden,
        latent,
        fresh_noise,
        timesteps,
        queue_slots,
        windows,
        mod_weight,
        attention_weight,
        jnp.transpose(final_weight),
    )
    return pl.pallas_call(
        by_token,
        out_shape=tuple(
            jax.ShapeDtypeStruct((T, F, x.shape[2]), BF16) for x in (out, pred, queue)
        ),
        in_specs=[vmem] * 3,
        out_specs=(vmem,) * 3,
    )(out, pred, queue)


def solution(mesh):
    placed = (
        P("seq", "queue", None),
        P("seq", "queue", None),
        P("seq", None),
        P("queue"),
        P(),
        P(),
        P(None, None, "seq"),
        P(None, "seq"),
        P(),
    )
    return jax.shard_map(
        functools.partial(shards, mesh.shape["queue"], mesh.shape["seq"]),
        mesh=mesh,
        in_specs=placed,
        out_specs=(P("seq", "queue", None), P("seq", "queue", None), P("seq", "queue", None)),
        check_vma=False,
    )
```

```python
import functools
import math

import jax
import jax.numpy as jnp
from jax import lax
from jax.experimental import pallas as pl
from jax.experimental.pallas import tpu as pltpu
from jax.sharding import PartitionSpec as P

HD = 128
STRIDE = 16
WMAX = 2

LN_EPS = 1e-06
DECAY = 2.3
NEAR_COST = 0.5

MESH = pl.DeviceIdType.MESH
F32 = jnp.float32
BF16 = jnp.bfloat16
NT = (((1,), (1,)), ((), ()))


def table(n, values):
    result = values[0]
    for k in range(1, len(values)):
        if values[k] != values[k - 1]:
            result = result + (values[k] - values[k - 1]) * ((n + len(values) - k) // len(values))
    return result


def kernel(
    Q,
    Z,
    hid_hbm,
    lat_hbm,
    fresh_hbm,
    steps_hbm,
    slots_hbm,
    wins_hbm,
    mw_hbm,
    w_hbm,
    fw_hbm,
    out,
    pred,
    queue,
    lat,
    fresh,
    steps,
    slots,
    wins,
    xs,
    own,
    wqkv,
    wout,
    mw,
    fw,
    part,
    mod,
    gate_part,
    gates_all,
    pattern,
    norm,
    qb,
    kv,
    hd,
    share,
    sent_r,
    sent_l,
    in_r,
    in_l,
    upd,
    got,
    small_sem,
    w_sem,
    mw_sem,
    fw_sem,
    mod_send,
    mod_recv,
    gate_send,
    gate_recv,
    ag_send,
    ag_recv,
    halo_send,
    halo_recv,
    rs_send,
    rs_recv,
    edge_send,
    edge_recv,
):
    T, F, D = hid_hbm.shape
    LH = w_hbm.shape[1] // (4 * HD)
    MP = mw_hbm.shape[2]
    FREQ = mw_hbm.shape[1]
    FRAMES = F * Q
    factor = 1.0 / math.sqrt(HD)
    z = lax.axis_index("seq")
    q = lax.axis_index("queue")
    z_right, z_left = lax.rem(z + 1, Z), lax.rem(z + Z - 1, Z)
    q_right, q_left = lax.rem(q + 1, Q), lax.rem(q + Q - 1, Q)

    def weight_copies():
        copies = []
        for h in range(LH):
            copies.append(
                pltpu.make_async_copy(
                    w_hbm.at[:, pl.ds(h * 4 * HD, 3 * HD)],
                    wqkv.at[:, pl.ds(h * 3 * HD, 3 * HD)],
                    w_sem.at[h],
                )
            )
        for h in range(LH):
            copies.append(
                pltpu.make_async_copy(
                    w_hbm.at[:, pl.ds(h * 4 * HD + 3 * HD, HD)],
                    wout.at[:, pl.ds(h * HD, HD)],
                    w_sem.at[LH + h],
                )
            )
        return copies

    barrier = pltpu.get_barrier_semaphore()
    for k in range(1, Z):
        pl.semaphore_signal(
            barrier, inc=1, device_id=(q, lax.rem(z + k, Z)), device_id_type=MESH
        )
    for other in (q_left, q_right):
        pl.semaphore_signal(barrier, inc=1, device_id=(other, z), device_id_type=MESH)

    weights = weight_copies()
    small = [
        pltpu.make_async_copy(src, dst, small_sem.at[i])
        for i, (src, dst) in enumerate(
            (
                (steps_hbm, steps),
                (slots_hbm, slots),
                (wins_hbm, wins),
                (lat_hbm, lat),
                (fresh_hbm, fresh),
                (hid_hbm, xs.at[z]),
            )
        )
    ]
    mw_copy = pltpu.make_async_copy(mw_hbm, mw, mw_sem)
    fw_copy = pltpu.make_async_copy(fw_hbm, fw, fw_sem)
    small[0].start()
    mw_copy.start()
    half = T // 2

    def piece(chunk, part_of):
        return xs.at[chunk, pl.ds(part_of * half, half)]

    def gather_copy(way, u, src, chunk, part_of):
        return pltpu.make_async_remote_copy(
            src_ref=src,
            dst_ref=piece(chunk, part_of),
            send_sem=ag_send.at[way, u],
            recv_sem=ag_recv.at[way, u],
            device_id=(q, z_right if way == 0 else z_left),
            device_id_type=MESH,
        )

    def own_copies(u):
        for way in (0, 1):
            part_of = u - 1 if way == 0 else 2 - u
            gather_copy(way, u, hid_hbm.at[pl.ds(part_of * half, half)], z, part_of).start()

    pl.semaphore_wait(barrier, Z + 1)
    own_copies(1)

    small[0].wait()
    rows = lax.broadcasted_iota(jnp.int32, (8, FREQ), 0)
    lanes = lax.broadcasted_iota(jnp.int32, (8, FREQ), 1)
    waves = FREQ // 2
    ladder = jnp.exp(lax.rem(lanes, waves).astype(F32) * (-math.log(10000.0) / waves))
    ids = jnp.where(lax.rem(rows, 2) == 0, steps[0], steps[1])
    angles = ids.astype(F32) * ladder
    freq = jnp.where(lanes < waves, jnp.cos(angles), jnp.sin(angles))
    temb = (freq / (1.0 + jnp.exp(-freq))).astype(BF16)
    mw_copy.wait()
    maps = [jnp.dot(temb, mw[p], preferred_element_type=F32) for p in range(3)]
    rows = lax.broadcasted_iota(jnp.int32, (8, MP), 0)
    pairs = jnp.where(rows < 2, maps[0], maps[1])
    my_columns = pl.ds(pl.multiple_of(z * MP, MP), MP)
    part[...] = pairs[: 2 * F]
    gate_part[...] = maps[2][:F]

    def mod_copy(k, owner):
        return pltpu.make_async_remote_copy(
            src_ref=part,
            dst_ref=mod.at[:, pl.ds(pl.multiple_of(owner * MP, MP), MP)],
            send_sem=mod_send.at[k],
            recv_sem=mod_recv.at[k],
            device_id=(q, lax.rem(z + k, Z)),
            device_id_type=MESH,
        )

    def gate_copy(k, owner):
        return pltpu.make_async_remote_copy(
            src_ref=gate_part,
            dst_ref=gates_all.at[:, pl.ds(pl.multiple_of(owner * MP, MP), MP)],
            send_sem=gate_send.at[k],
            recv_sem=gate_recv.at[k],
            device_id=(q, lax.rem(z + k, Z)),
            device_id_type=MESH,
        )

    for k in range(1, Z):
        mod_copy(k, z).start()
    own_copies(2)
    for copy in small[1:] + weights + [fw_copy]:
        copy.start()
    mod[:, my_columns] = part[...]
    gates_all[:, my_columns] = gate_part[...]
    in_r[0] = jnp.zeros((T, D), BF16)
    in_l[0] = jnp.zeros((T, D), BF16)

    def choice(rows_count, column_of):
        rows = lax.broadcasted_iota(jnp.int32, (rows_count, rows_count), 0)
        cols = lax.broadcasted_iota(jnp.int32, (rows_count, rows_count), 1)
        return (cols == column_of(rows)).astype(BF16)

    for copy in small[1:]:
        copy.wait()
    by_frame = choice(F * T, lambda r: F * lax.rem(r, T) + lax.div(r, T))
    own_rows = jnp.dot(by_frame, xs[z].reshape(F * T, D), preferred_element_type=F32).astype(BF16)
    for f in range(F):
        own[f] = own_rows[f * T : (f + 1) * T]

    def pass_on(u):
        places = gather_place(u)
        for way in (0, 1):
            chunk, part_of = places[way]
            gather_copy(way, u, piece(chunk, part_of), chunk, part_of).wait_recv()

            @pl.when(u + 2 <= Z - 1)
            def _():
                gather_copy(way, u + 2, piece(chunk, part_of), chunk, part_of).start()

    def gather_place(u):
        step = (u + 1) // 2
        left = (lax.rem(z + Z - step, Z), lax.rem(u + 1, 2))
        right = (lax.rem(z + step, Z), lax.rem(u, 2))
        return left, right

    pass_on(1)
    for k in range(1, Z):
        mod_copy(k, lax.rem(z + Z - k, Z)).wait_recv()
    rows = lax.broadcasted_iota(jnp.int32, (8, D), 0)
    for p in (0, 1):
        pattern[p] = jnp.where(
            lax.rem(rows, 2) == 0, mod[2 * p : 2 * p + 1, :], mod[2 * p + 1 : 2 * p + 2, :]
        ) + float(p)
    for copy in weights:
        copy.wait()

    def normalise(chunk, part_of, base):
        for r in range(0, half, 8):
            x = xs[chunk, pl.ds(part_of * half + r, 8)].reshape(16, D).astype(F32)
            centred = x - jnp.sum(x, axis=1, keepdims=True) * (1.0 / D)
            variance = jnp.sum(centred * centred, axis=1, keepdims=True) * (1.0 / D)
            y = (centred * lax.rsqrt(variance + LN_EPS)).reshape(2, 8, D)
            y = y * pattern[1][None] + pattern[0][None]
            norm[base + F * r : base + F * r + 16, :] = y.reshape(16, D).astype(BF16)

    def token_rows(chunk, part_of):
        return pl.ds(pl.multiple_of(chunk * T + part_of * half, half), half)

    def halo_copy(side, u, i, chunk, part_of):
        rows_here = token_rows(chunk, part_of)
        return pltpu.make_async_remote_copy(
            src_ref=kv.at[pl.ds(F, F), rows_here],
            dst_ref=kv.at[pl.ds(0 if side == 0 else 2 * F, F), rows_here],
            send_sem=halo_send.at[side, i, u],
            recv_sem=halo_recv.at[side, i, u],
            device_id=(q_right if side == 0 else q_left, z),
            device_id_type=MESH,
        )

    split = choice(
        2 * T,
        lambda r: lax.rem(lax.div(r, half), 2) * T + F * lax.rem(r, half) + lax.div(r, T),
    )

    def halo_wait(u):
        places = gather_place(u)
        for way in (0, 1):
            for side in (0, 1):
                halo_copy(side, u, way, *places[way]).wait_recv()

    def gather_unit(u, carry):
        places = gather_place(u)
        pl.when(u >= 2)(lambda: pass_on(u))

        for way in (0, 1):
            normalise(*places[way], way * T)
        mixed_rows = jnp.dot(norm[...], wqkv[...], preferred_element_type=F32).astype(BF16)
        projected = jnp.dot(split, mixed_rows, preferred_element_type=F32).astype(BF16)
        for way in (0, 1):
            rows_here = token_rows(*places[way])
            for f in range(F):
                at_row = f * T + way * half
                block = projected[at_row : at_row + half]
                for h in range(LH):
                    at = h * 3 * HD
                    qb[f, rows_here, h * HD : (h + 1) * HD] = block[:, at : at + HD]
                    kv[F + f, rows_here, h * 2 * HD : (h + 1) * 2 * HD] = block[
                        :, at + HD : at + 3 * HD
                    ]
            for side in (0, 1):
                halo_copy(side, u, way, *places[way]).start()

        @pl.when(u >= 2)
        def _():
            halo_wait(u - 2)

        return carry

    lax.fori_loop(0, Z, gather_unit, 0)
    for k in range(1, Z):
        gate_copy(k, z).start()

    def spatial(pieces):
        each = [(chunk, frame, h) for chunk, frame in pieces for h in range(LH)]
        scores = [
            lax.dot_general(
                qb[frame, pl.ds(pl.multiple_of(chunk * T, T), T), h * HD : (h + 1) * HD],
                kv[F + frame, :, h * 2 * HD : h * 2 * HD + HD],
                NT,
                preferred_element_type=F32,
            )
            for chunk, frame, h in each
        ]
        scores = [score * factor for score in scores]
        peaks = [jnp.max(score, axis=1, keepdims=True) for score in scores]
        expos = [jnp.exp(score - peak) for score, peak in zip(scores, peaks)]
        totals = [jnp.sum(expo, axis=1, keepdims=True) for expo in expos]
        mixed = [
            jnp.dot(
                expo.astype(BF16),
                kv[F + frame, :, h * 2 * HD + HD : (h + 1) * 2 * HD],
                preferred_element_type=F32,
            )
            for expo, (chunk, frame, h) in zip(expos, each)
        ]
        results = [m / total for m, total in zip(mixed, totals)]
        return [results[:LH], results[LH:]]

    def temporal(chunk, frame):
        rows_here = pl.ds(pl.multiple_of(chunk * T, T), T)
        here = q * F + frame
        slot = slots[here]
        window = wins[here]
        gates = []
        for d in range(-WMAX, WMAX + 1):
            there = here + d
            inside = jnp.logical_and(there >= 0, there < FRAMES)
            gap = jnp.abs(slots[jnp.clip(there, 0, FRAMES - 1)] - slot)
            gates.append((jnp.logical_and(inside, gap <= window), gap.astype(F32) * NEAR_COST))
        results = []
        for h in range(LH):
            queries = qb[frame, rows_here, h * HD : (h + 1) * HD].astype(F32)
            logits = []
            for d in range(2 * WMAX + 1):
                keys = kv[F + frame + d - WMAX, rows_here, h * 2 * HD : h * 2 * HD + HD]
                score = jnp.sum(queries * keys.astype(F32), axis=1, keepdims=True) * factor
                allowed, cost = gates[d]
                logits.append(jnp.where(allowed, score - cost, -1e30))
            peak = functools.reduce(jnp.maximum, logits)
            total = jnp.zeros((T, 1), F32)
            mixed = jnp.zeros((T, HD), F32)
            for d in range(2 * WMAX + 1):
                weight = jnp.where(gates[d][0], jnp.exp(logits[d] - peak), 0.0)
                values = kv[
                    F + frame + d - WMAX, rows_here, h * 2 * HD + HD : (h + 1) * 2 * HD
                ]
                total = total + weight
                mixed = mixed + weight * values.astype(F32)
            results.append(mixed / total)
        return results

    def scatter_copy(way, n, part_of):
        src, dst = (sent_r, in_r) if way == 0 else (sent_l, in_l)
        rows_here = pl.ds(part_of * half, half)
        return pltpu.make_async_remote_copy(
            src_ref=src.at[n - 1, rows_here],
            dst_ref=dst.at[n, rows_here],
            send_sem=rs_send.at[way, part_of, n],
            recv_sem=rs_recv.at[way, part_of, n],
            device_id=(q, z_right if way == 0 else z_left),
            device_id_type=MESH,
        )

    def scatter_unit(n, carry):
        right_step = table(n, (0, 3, 4, 2, 3, 2, 1, 1, 0))
        left_step = table(n, (0, 3, 4, 2, 3, 1, 2, 1, 0))
        right = (lax.rem(z + right_step, Z), table(n, (1, 1, 0, 1, 0, 0, 0, 1, 1)))
        left = (lax.rem(z + Z - left_step, Z), table(n, (0, 0, 1, 0, 1, 0, 1, 1, 0)))
        spread = spatial([right, left])

        @pl.when(n == 1)
        def _():
            halo_wait(Z - 2)

        @pl.when(n == 2)
        def _():
            halo_wait(Z - 1)

        along = [temporal(*right), temporal(*left)]
        for i in (0, 1):
            for h in range(LH):
                hd[i * T : (i + 1) * T, h * HD : (h + 1) * HD] = (
                    spread[i][h] + along[i][h]
                ).astype(BF16)
        tile = 512
        for c in range(0, D, tile):
            share[:, c : c + tile] = lax.dot_general(
                hd[...], wout[c : c + tile, :], NT, preferred_element_type=F32
            )

        @pl.when(n <= Z - 1)
        def _():
            needs = (
                table(n, (0, 0, 0, 1, 2, 4, 5, 3, 0)),
                table(n, (0, 0, 0, 1, 2, 3, 4, 6, 0)),
            )
            for part_of in (0, 1):
                for way, (sent, arrived) in enumerate(((sent_r, in_r), (sent_l, in_l))):
                    need = needs[way]

                    @pl.when(n >= 3)
                    def _():
                        scatter_copy(way, need, part_of).wait_recv()

                    mine = way * T + part_of * half
                    rows_here = slice(part_of * half, (part_of + 1) * half)
                    sent[n - 1, rows_here, :] = (
                        share[mine : mine + half, :] + arrived[need, rows_here, :].astype(F32)
                    ).astype(BF16)
                    scatter_copy(way, n, part_of).start()

        @pl.when(n >= 2)
        def _():
            u = n - 1
            places = gather_place(u)
            for way in (0, 1):
                gather_copy(way, u, piece(*places[way]), *places[way]).wait_send()

        @pl.when(n >= 3)
        def _():
            for way in (0, 1):
                for part_of in (0, 1):
                    scatter_copy(way, n - 2, part_of).wait_send()

        halo_places = gather_place(n - 1)
        for way in (0, 1):
            for side in (0, 1):
                halo_copy(side, n - 1, way, *halo_places[way]).wait_send()
        return carry

    lax.fori_loop(1, Z + 1, scatter_unit, 0)

    fw_copy.wait()
    for k in range(1, Z):
        gate_copy(k, lax.rem(z + Z - k, Z)).wait_recv()
        gate_copy(k, z).wait_send()
        mod_copy(k, z).wait_send()
    horizon = STRIDE * (FRAMES + 1)
    LAT = lat.shape[2]

    def schedule(f):
        ids = jnp.full((T, LAT), steps[f], jnp.int32)
        now = jnp.exp(ids.astype(F32) * (-DECAY / horizon))
        before = jnp.exp((ids - STRIDE).astype(F32) * (-DECAY / horizon))
        return jnp.sqrt(1.0 - now), jnp.sqrt(now), jnp.sqrt(before), jnp.sqrt(1.0 - before)

    tables = [schedule(f) for f in range(F)]
    edge = pltpu.make_async_remote_copy(
        src_ref=upd,
        dst_ref=got,
        send_sem=edge_send,
        recv_sem=edge_recv,
        device_id=(q_left, z),
        device_id_type=MESH,
    )
    last = ((6, 5), (7, 7))
    for f in range(F):
        for way in (0, 1):
            for part_of in (0, 1):
                scatter_copy(way, last[f][way], part_of).wait_recv()
        mine = (1 - f) * T
        total = (
            share[mine : mine + T, :]
            + in_r[last[f][0]].astype(F32)
            + in_l[last[f][1]].astype(F32)
        )
        gate = gates_all[f : f + 1, :]
        block = (own[f].astype(F32) + gate * total).astype(BF16)
        out[f] = block
        noise = lax.dot_general(block, fw[...], NT, preferred_element_type=F32)
        pred[f] = noise.astype(BF16)
        noise_now, root_now, root_before, noise_before = tables[f]
        clean = (lat[:, f, :].astype(F32) - noise_now * noise) / root_now
        updated = (root_before * clean + noise_before * noise).astype(BF16)
        if f == 0:
            upd[...] = updated
            edge.start()
        else:
            queue[f - 1] = updated
    edge.wait_recv()
    queue[F - 1] = jnp.where(q == Q - 1, fresh[...], got[...])

    edge.wait_send()
    for way in (0, 1):
        for part_of in (0, 1):
            scatter_copy(way, Z - 1, part_of).wait_send()


def by_token(*refs):
    for src, dst in zip(refs[:3], refs[3:]):
        for f in range(src.shape[0]):
            dst[:, f, :] = src[f]


def shards(
    Q,
    Z,
    hidden,
    latent,
    fresh_noise,
    timesteps,
    queue_slots,
    windows,
    mod_weight,
    attention_weight,
    final_weight,
):
    T, F, D = hidden.shape
    LAT = latent.shape[2]
    W = attention_weight.shape[1]
    MP = mod_weight.shape[2]
    vmem = pl.BlockSpec(memory_space=pltpu.VMEM)
    hbm = pl.BlockSpec(memory_space=pltpu.HBM)
    dma = pltpu.SemaphoreType.DMA
    out, pred, queue = pl.pallas_call(
        functools.partial(kernel, Q, Z),
        out_shape=(
            jax.ShapeDtypeStruct((F, T, D), BF16),
            jax.ShapeDtypeStruct((F, T, LAT), BF16),
            jax.ShapeDtypeStruct((F, T, LAT), BF16),
        ),
        in_specs=[hbm] * 9,
        out_specs=(vmem, vmem, vmem),
        scratch_shapes=[
            pltpu.VMEM(latent.shape, BF16),
            pltpu.VMEM(fresh_noise.shape, BF16),
            pltpu.SMEM(timesteps.shape, jnp.int32),
            pltpu.SMEM(queue_slots.shape, jnp.int32),
            pltpu.SMEM(windows.shape, jnp.int32),
            pltpu.VMEM((Z, T, F, D), BF16),
            pltpu.VMEM((F, T, D), BF16),
            pltpu.VMEM((D, W // 4 * 3), BF16),
            pltpu.VMEM((D, W // 4), BF16),
            pltpu.VMEM(mod_weight.shape, BF16),
            pltpu.VMEM((LAT, D), BF16),
            pltpu.VMEM((2 * F, MP), F32),
            pltpu.VMEM((2 * F, D), F32),
            pltpu.VMEM((F, MP), F32),
            pltpu.VMEM((F, D), F32),
            pltpu.VMEM((2, 8, D), F32),
            pltpu.VMEM((2 * T, D), BF16),
            pltpu.VMEM((F, Z * T, W // 4), BF16),
            pltpu.VMEM((3 * F, Z * T, W // 2), BF16),
            pltpu.VMEM((2 * T, W // 4), BF16),
            pltpu.VMEM((2 * T, D), F32),
            pltpu.VMEM((Z - 1, T, D), BF16),
            pltpu.VMEM((Z - 1, T, D), BF16),
            pltpu.VMEM((Z, T, D), BF16),
            pltpu.VMEM((Z, T, D), BF16),
            pltpu.VMEM((T, LAT), BF16),
            pltpu.VMEM((T, LAT), BF16),
            dma((6,)),
            dma((2 * (W // (4 * HD)),)),
            dma,
            dma,
            dma((Z,)),
            dma((Z,)),
            dma((Z,)),
            dma((Z,)),
            dma((2, Z)),
            dma((2, Z)),
            dma((2, 2, Z)),
            dma((2, 2, Z)),
            dma((2, 2, Z)),
            dma((2, 2, Z)),
            dma,
            dma,
        ],
        compiler_params=pltpu.CompilerParams(
            collective_id=0, has_side_effects=True, vmem_limit_bytes=56 * 1024 * 1024
        ),
        cost_estimate=pl.CostEstimate(
            flops=2 * Z * T * F * D * W, bytes_accessed=2 * D * W, transcendentals=0
        ),
    )(
        hidden,
        latent,
        fresh_noise,
        timesteps,
        queue_slots,
        windows,
        mod_weight,
        attention_weight,
        jnp.transpose(final_weight),
    )
    return pl.pallas_call(
        by_token,
        out_shape=tuple(
            jax.ShapeDtypeStruct((T, F, x.shape[2]), BF16) for x in (out, pred, queue)
        ),
        in_specs=[vmem] * 3,
        out_specs=(vmem,) * 3,
    )(out, pred, queue)


def solution(mesh):
    placed = (
        P("seq", "queue", None),
        P("seq", "queue", None),
        P("seq", None),
        P("queue"),
        P(),
        P(),
        P(None, None, "seq"),
        P(None, "seq"),
        P(),
    )
    return jax.shard_map(
        functools.partial(shards, mesh.shape["queue"], mesh.shape["seq"]),
        mesh=mesh,
        in_specs=placed,
        out_specs=(P("seq", "queue", None), P("seq", "queue", None), P("seq", "queue", None)),
        check_vma=False,
    )
```

```python
import functools
import math

import jax
import jax.numpy as jnp
from jax import lax
from jax.experimental import pallas as pl
from jax.experimental.pallas import tpu as pltpu
from jax.sharding import PartitionSpec as P

HD = 128
STRIDE = 16
WMAX = 2

LN_EPS = 1e-06
DECAY = 2.3
NEAR_COST = 0.5

MESH = pl.DeviceIdType.MESH
F32 = jnp.float32
BF16 = jnp.bfloat16
NT = (((1,), (1,)), ((), ()))


def table(n, values):
    result = values[0]
    for k in range(1, len(values)):
        if values[k] != values[k - 1]:
            result = result + (values[k] - values[k - 1]) * ((n + len(values) - k) // len(values))
    return result


def kernel(
    Q,
    Z,
    hid_hbm,
    lat_hbm,
    fresh_hbm,
    steps_hbm,
    slots_hbm,
    wins_hbm,
    mw_hbm,
    w_hbm,
    fw_hbm,
    out,
    pred,
    queue,
    lat,
    fresh,
    steps,
    slots,
    wins,
    xs,
    own,
    wq,
    wkv,
    wout,
    wout_turned,
    mw,
    fw,
    part,
    mod,
    gate_part,
    gates_all,
    pattern,
    norm,
    qb,
    kv,
    hd,
    share,
    sent_r,
    sent_l,
    in_r,
    in_l,
    upd,
    got,
    small_sem,
    w_sem,
    mw_sem,
    fw_sem,
    mod_send,
    mod_recv,
    gate_send,
    gate_recv,
    ag_send,
    ag_recv,
    halo_send,
    halo_recv,
    rs_send,
    rs_recv,
    edge_send,
    edge_recv,
):
    T, F, D = hid_hbm.shape
    LH = w_hbm.shape[1] // (4 * HD)
    MP = mw_hbm.shape[2]
    FREQ = mw_hbm.shape[1]
    FRAMES = F * Q
    factor = 1.0 / math.sqrt(HD)
    z = lax.axis_index("seq")
    q = lax.axis_index("queue")
    z_right, z_left = lax.rem(z + 1, Z), lax.rem(z + Z - 1, Z)
    q_right, q_left = lax.rem(q + 1, Q), lax.rem(q + Q - 1, Q)

    def weight_copies():
        copies = []
        for target, first, width in ((wkv, HD, 2 * HD), (wq, 0, HD), (wout, 3 * HD, HD)):
            for h in range(LH):
                copies.append(
                    pltpu.make_async_copy(
                        w_hbm.at[:, pl.ds(h * 4 * HD + first, width)],
                        target.at[:, pl.ds(h * width, width)],
                        w_sem.at[len(copies)],
                    )
                )
        return copies

    barrier = pltpu.get_barrier_semaphore()
    for k in range(1, Z):
        pl.semaphore_signal(
            barrier, inc=1, device_id=(q, lax.rem(z + k, Z)), device_id_type=MESH
        )
    for other in (q_left, q_right):
        pl.semaphore_signal(barrier, inc=1, device_id=(other, z), device_id_type=MESH)

    weights = weight_copies()
    small = [
        pltpu.make_async_copy(src, dst, small_sem.at[i])
        for i, (src, dst) in enumerate(
            (
                (steps_hbm, steps),
                (slots_hbm, slots),
                (wins_hbm, wins),
                (lat_hbm, lat),
                (fresh_hbm, fresh),
                (hid_hbm, xs.at[z]),
            )
        )
    ]
    mw_copy = pltpu.make_async_copy(mw_hbm, mw, mw_sem)
    fw_copy = pltpu.make_async_copy(fw_hbm, fw, fw_sem)
    small[0].start()
    mw_copy.start()
    half = T // 2

    def piece(chunk, part_of):
        return xs.at[chunk, pl.ds(part_of * half, half)]

    def gather_copy(way, u, src, chunk, part_of):
        return pltpu.make_async_remote_copy(
            src_ref=src,
            dst_ref=piece(chunk, part_of),
            send_sem=ag_send.at[way, u],
            recv_sem=ag_recv.at[way, u],
            device_id=(q, z_right if way == 0 else z_left),
            device_id_type=MESH,
        )

    def own_copies(u):
        for way in (0, 1):
            part_of = u - 1 if way == 0 else 2 - u
            gather_copy(way, u, hid_hbm.at[pl.ds(part_of * half, half)], z, part_of).start()

    pl.semaphore_wait(barrier, Z + 1)
    own_copies(1)

    small[0].wait()
    rows = lax.broadcasted_iota(jnp.int32, (8, FREQ), 0)
    lanes = lax.broadcasted_iota(jnp.int32, (8, FREQ), 1)
    waves = FREQ // 2
    ladder = jnp.exp(lax.rem(lanes, waves).astype(F32) * (-math.log(10000.0) / waves))
    ids = jnp.where(lax.rem(rows, 2) == 0, steps[0], steps[1])
    angles = ids.astype(F32) * ladder
    freq = jnp.where(lanes < waves, jnp.cos(angles), jnp.sin(angles))
    temb = (freq / (1.0 + jnp.exp(-freq))).astype(BF16)
    mw_copy.wait()
    maps = [jnp.dot(temb, mw[p], preferred_element_type=F32) for p in range(3)]
    rows = lax.broadcasted_iota(jnp.int32, (8, MP), 0)
    pairs = jnp.where(rows < 2, maps[0], maps[1])
    my_columns = pl.ds(pl.multiple_of(z * MP, MP), MP)
    part[...] = pairs[: 2 * F]
    gate_part[...] = maps[2][:F]

    def mod_copy(k, owner):
        return pltpu.make_async_remote_copy(
            src_ref=part,
            dst_ref=mod.at[:, pl.ds(pl.multiple_of(owner * MP, MP), MP)],
            send_sem=mod_send.at[k],
            recv_sem=mod_recv.at[k],
            device_id=(q, lax.rem(z + k, Z)),
            device_id_type=MESH,
        )

    def gate_copy(k, owner):
        return pltpu.make_async_remote_copy(
            src_ref=gate_part,
            dst_ref=gates_all.at[:, pl.ds(pl.multiple_of(owner * MP, MP), MP)],
            send_sem=gate_send.at[k],
            recv_sem=gate_recv.at[k],
            device_id=(q, lax.rem(z + k, Z)),
            device_id_type=MESH,
        )

    for k in range(1, Z):
        mod_copy(k, z).start()
    own_copies(2)
    for copy in small[1:] + weights + [fw_copy]:
        copy.start()
    mod[:, my_columns] = part[...]
    gates_all[:, my_columns] = gate_part[...]
    in_r[0] = jnp.zeros((T, D), BF16)
    in_l[0] = jnp.zeros((T, D), BF16)

    def choice(rows_count, column_of):
        rows = lax.broadcasted_iota(jnp.int32, (rows_count, rows_count), 0)
        cols = lax.broadcasted_iota(jnp.int32, (rows_count, rows_count), 1)
        return (cols == column_of(rows)).astype(BF16)

    for copy in small[1:]:
        copy.wait()
    by_frame = choice(F * T, lambda r: F * lax.rem(r, T) + lax.div(r, T))
    own_rows = jnp.dot(by_frame, xs[z].reshape(F * T, D), preferred_element_type=F32).astype(BF16)
    for f in range(F):
        own[f] = own_rows[f * T : (f + 1) * T]

    def pass_on(u):
        places = gather_place(u)
        for way in (0, 1):
            chunk, part_of = places[way]
            gather_copy(way, u, piece(chunk, part_of), chunk, part_of).wait_recv()

            @pl.when(u + 2 <= Z - 1)
            def _():
                gather_copy(way, u + 2, piece(chunk, part_of), chunk, part_of).start()

    def gather_place(u):
        step = (u + 1) // 2
        left = (lax.rem(z + Z - step, Z), lax.rem(u + 1, 2))
        right = (lax.rem(z + step, Z), lax.rem(u, 2))
        return left, right

    pass_on(1)
    for k in range(1, Z):
        mod_copy(k, lax.rem(z + Z - k, Z)).wait_recv()
    rows = lax.broadcasted_iota(jnp.int32, (8, D), 0)
    for p in (0, 1):
        pattern[p] = jnp.where(
            lax.rem(rows, 2) == 0, mod[2 * p : 2 * p + 1, :], mod[2 * p + 1 : 2 * p + 2, :]
        ) + float(p)
    for copy in weights:
        copy.wait()
    same = choice(LH * HD, lambda r: r)
    tile = 512
    for c in range(0, D, tile):
        wout_turned[:, c : c + tile] = lax.dot_general(
            same, wout[c : c + tile, :], NT, preferred_element_type=F32
        ).astype(BF16)

    def normalise(chunk, part_of, base):
        for r in range(0, half, 8):
            x = xs[chunk, pl.ds(part_of * half + r, 8)].reshape(16, D).astype(F32)
            centred = x - jnp.sum(x, axis=1, keepdims=True) * (1.0 / D)
            variance = jnp.sum(centred * centred, axis=1, keepdims=True) * (1.0 / D)
            y = (centred * lax.rsqrt(variance + LN_EPS)).reshape(2, 8, D)
            y = y * pattern[1][None] + pattern[0][None]
            norm[base + F * r : base + F * r + 16, :] = y.reshape(16, D).astype(BF16)

    def token_rows(chunk, part_of):
        return pl.ds(pl.multiple_of(chunk * T + part_of * half, half), half)

    def halo_copy(side, u, i, chunk, part_of):
        rows_here = token_rows(chunk, part_of)
        return pltpu.make_async_remote_copy(
            src_ref=kv.at[pl.ds(F, F), rows_here],
            dst_ref=kv.at[pl.ds(0 if side == 0 else 2 * F, F), rows_here],
            send_sem=halo_send.at[side, i, u],
            recv_sem=halo_recv.at[side, i, u],
            device_id=(q_right if side == 0 else q_left, z),
            device_id_type=MESH,
        )

    split = choice(
        2 * T,
        lambda r: lax.rem(lax.div(r, half), 2) * T + F * lax.rem(r, half) + lax.div(r, T),
    )

    def halo_wait(u):
        places = gather_place(u)
        for way in (0, 1):
            for side in (0, 1):
                halo_copy(side, u, way, *places[way]).wait_recv()

    def project(weight):
        mixed_rows = jnp.dot(norm[...], weight[...], preferred_element_type=F32).astype(BF16)
        return jnp.dot(split, mixed_rows, preferred_element_type=F32).astype(BF16)

    def keep_queries(u):
        places = gather_place(u)
        projected = project(wq)
        for way in (0, 1):
            rows_here = token_rows(*places[way])
            for f in range(F):
                at_row = f * T + way * half
                qb[f, rows_here, :] = projected[at_row : at_row + half]

    def gather_unit(u, carry):
        places = gather_place(u)
        pl.when(u >= 2)(lambda: pass_on(u))

        for way in (0, 1):
            normalise(*places[way], way * T)
        projected = project(wkv)
        for way in (0, 1):
            rows_here = token_rows(*places[way])
            for f in range(F):
                at_row = f * T + way * half
                kv[F + f, rows_here, :] = projected[at_row : at_row + half]
            for side in (0, 1):
                halo_copy(side, u, way, *places[way]).start()

        @pl.when(u < Z - 1)
        def _():
            keep_queries(u)

        @pl.when(u >= 2)
        def _():
            halo_wait(u - 2)

        return carry

    lax.fori_loop(0, Z, gather_unit, 0)
    for k in range(1, Z):
        gate_copy(k, z).start()

    def spatial(pieces):
        each = [(chunk, frame, h) for chunk, frame in pieces for h in range(LH)]
        scores = [
            lax.dot_general(
                qb[frame, pl.ds(pl.multiple_of(chunk * T, T), T), h * HD : (h + 1) * HD],
                kv[F + frame, :, h * 2 * HD : h * 2 * HD + HD],
                NT,
                preferred_element_type=F32,
            )
            for chunk, frame, h in each
        ]
        scores = [score * factor for score in scores]
        peaks = [jnp.max(score, axis=1, keepdims=True) for score in scores]
        expos = [jnp.exp(score - peak) for score, peak in zip(scores, peaks)]
        totals = [jnp.sum(expo, axis=1, keepdims=True) for expo in expos]
        mixed = [
            jnp.dot(
                expo.astype(BF16),
                kv[F + frame, :, h * 2 * HD + HD : (h + 1) * 2 * HD],
                preferred_element_type=F32,
            )
            for expo, (chunk, frame, h) in zip(expos, each)
        ]
        results = [m / total for m, total in zip(mixed, totals)]
        return [results[:LH], results[LH:]]

    def temporal(chunk, frame):
        rows_here = pl.ds(pl.multiple_of(chunk * T, T), T)
        here = q * F + frame
        slot = slots[here]
        window = wins[here]
        gates = []
        for d in range(-WMAX, WMAX + 1):
            there = here + d
            inside = jnp.logical_and(there >= 0, there < FRAMES)
            gap = jnp.abs(slots[jnp.clip(there, 0, FRAMES - 1)] - slot)
            gates.append((jnp.logical_and(inside, gap <= window), gap.astype(F32) * NEAR_COST))
        results = []
        for h in range(LH):
            queries = qb[frame, rows_here, h * HD : (h + 1) * HD].astype(F32)
            logits = []
            for d in range(2 * WMAX + 1):
                keys = kv[F + frame + d - WMAX, rows_here, h * 2 * HD : h * 2 * HD + HD]
                score = jnp.sum(queries * keys.astype(F32), axis=1, keepdims=True) * factor
                allowed, cost = gates[d]
                logits.append(jnp.where(allowed, score - cost, -1e30))
            peak = functools.reduce(jnp.maximum, logits)
            total = jnp.zeros((T, 1), F32)
            mixed = jnp.zeros((T, HD), F32)
            for d in range(2 * WMAX + 1):
                weight = jnp.where(gates[d][0], jnp.exp(logits[d] - peak), 0.0)
                values = kv[
                    F + frame + d - WMAX, rows_here, h * 2 * HD + HD : (h + 1) * 2 * HD
                ]
                total = total + weight
                mixed = mixed + weight * values.astype(F32)
            results.append(mixed / total)
        return results

    def scatter_copy(way, n, part_of):
        src, dst = (sent_r, in_r) if way == 0 else (sent_l, in_l)
        rows_here = pl.ds(part_of * half, half)
        return pltpu.make_async_remote_copy(
            src_ref=src.at[n - 1, rows_here],
            dst_ref=dst.at[n, rows_here],
            send_sem=rs_send.at[way, part_of, n],
            recv_sem=rs_recv.at[way, part_of, n],
            device_id=(q, z_right if way == 0 else z_left),
            device_id_type=MESH,
        )

    def drain(u, carry):
        places = gather_place(u)
        for way in (0, 1):

            @pl.when(u >= 1)
            def _():
                gather_copy(way, u, piece(*places[way]), *places[way]).wait_send()

            for side in (0, 1):
                halo_copy(side, u, way, *places[way]).wait_send()
        return carry

    def sent_off(n, carry):
        for way in (0, 1):
            for part_of in (0, 1):
                scatter_copy(way, n, part_of).wait_send()
        return carry

    own_turn = Z // 2

    def scatter_unit(m, carry):
        n = table(m, (0, 1, 2, 3, 0, 4, 5, 6, 7))
        right_step = table(m, (0, 3, 4, 2, 0, 3, 2, 1, 1))
        left_step = table(m, (0, 3, 4, 2, 0, 3, 1, 2, 1))
        right = (lax.rem(z + right_step, Z), table(m, (1, 1, 0, 1, 1, 0, 0, 0, 1)))
        left = (lax.rem(z + Z - left_step, Z), table(m, (0, 0, 1, 0, 0, 1, 0, 1, 1)))
        place = table(m, (0, 0, 0, 0, 1, 0, 0, 0, 0))

        @pl.when(m == 2)
        def _():
            keep_queries(Z - 1)

        spread = spatial([right, left])

        @pl.when(m == 1)
        def _():
            halo_wait(Z - 2)

        @pl.when(m == 2)
        def _():
            halo_wait(Z - 1)

        along = [temporal(*right), temporal(*left)]
        for i in (0, 1):
            for h in range(LH):
                hd[i * T : (i + 1) * T, h * HD : (h + 1) * HD] = (
                    spread[i][h] + along[i][h]
                ).astype(BF16)
        for c in range(0, D, tile):
            share[place, :, c : c + tile] = jnp.dot(
                hd[...], wout_turned[:, c : c + tile], preferred_element_type=F32
            )

        @pl.when(m != own_turn)
        def _():
            needs = (
                table(m, (0, 0, 0, 1, 0, 2, 4, 5, 3)),
                table(m, (0, 0, 0, 1, 0, 2, 3, 4, 6)),
            )
            for part_of in (0, 1):
                for way, (sent, arrived) in enumerate(((sent_r, in_r), (sent_l, in_l))):
                    need = needs[way]

                    @pl.when(m >= 3)
                    def _():
                        scatter_copy(way, need, part_of).wait_recv()

                    mine = way * T + part_of * half
                    rows_here = slice(part_of * half, (part_of + 1) * half)
                    sent[n - 1, rows_here, :] = (
                        share[0, mine : mine + half, :]
                        + arrived[need, rows_here, :].astype(F32)
                    ).astype(BF16)
                    scatter_copy(way, n, part_of).start()

        @pl.when(m == own_turn)
        def _():
            lax.fori_loop(0, Z, drain, 0)

        return carry

    lax.fori_loop(1, Z + 1, scatter_unit, 0)

    lax.fori_loop(1, Z - 2, sent_off, 0)
    fw_copy.wait()
    for k in range(1, Z):
        gate_copy(k, lax.rem(z + Z - k, Z)).wait_recv()
        gate_copy(k, z).wait_send()
        mod_copy(k, z).wait_send()
    horizon = STRIDE * (FRAMES + 1)
    LAT = lat.shape[2]

    def schedule(f):
        ids = jnp.full((T, LAT), steps[f], jnp.int32)
        now = jnp.exp(ids.astype(F32) * (-DECAY / horizon))
        before = jnp.exp((ids - STRIDE).astype(F32) * (-DECAY / horizon))
        return jnp.sqrt(1.0 - now), jnp.sqrt(now), jnp.sqrt(before), jnp.sqrt(1.0 - before)

    tables = [schedule(f) for f in range(F)]
    edge = pltpu.make_async_remote_copy(
        src_ref=upd,
        dst_ref=got,
        send_sem=edge_send,
        recv_sem=edge_recv,
        device_id=(q_left, z),
        device_id_type=MESH,
    )
    last = ((6, 5), (7, 7))
    for f in range(F):
        for way in (0, 1):
            for part_of in (0, 1):
                scatter_copy(way, last[f][way], part_of).wait_recv()
        mine = (1 - f) * T
        total = (
            share[1, mine : mine + T, :]
            + in_r[last[f][0]].astype(F32)
            + in_l[last[f][1]].astype(F32)
        )
        gate = gates_all[f : f + 1, :]
        block = (own[f].astype(F32) + gate * total).astype(BF16)
        out[f] = block
        noise = lax.dot_general(block, fw[...], NT, preferred_element_type=F32)
        pred[f] = noise.astype(BF16)
        noise_now, root_now, root_before, noise_before = tables[f]
        clean = (lat[:, f, :].astype(F32) - noise_now * noise) / root_now
        updated = (root_before * clean + noise_before * noise).astype(BF16)
        if f == 0:
            upd[...] = updated
            edge.start()
        else:
            queue[f - 1] = updated
    edge.wait_recv()
    queue[F - 1] = jnp.where(q == Q - 1, fresh[...], got[...])

    edge.wait_send()
    lax.fori_loop(Z - 2, Z, sent_off, 0)


def by_token(*refs):
    for src, dst in zip(refs[:3], refs[3:]):
        for f in range(src.shape[0]):
            dst[:, f, :] = src[f]


def shards(
    Q,
    Z,
    hidden,
    latent,
    fresh_noise,
    timesteps,
    queue_slots,
    windows,
    mod_weight,
    attention_weight,
    final_weight,
):
    T, F, D = hidden.shape
    LAT = latent.shape[2]
    W = attention_weight.shape[1]
    MP = mod_weight.shape[2]
    vmem = pl.BlockSpec(memory_space=pltpu.VMEM)
    hbm = pl.BlockSpec(memory_space=pltpu.HBM)
    dma = pltpu.SemaphoreType.DMA
    out, pred, queue = pl.pallas_call(
        functools.partial(kernel, Q, Z),
        out_shape=(
            jax.ShapeDtypeStruct((F, T, D), BF16),
            jax.ShapeDtypeStruct((F, T, LAT), BF16),
            jax.ShapeDtypeStruct((F, T, LAT), BF16),
        ),
        in_specs=[hbm] * 9,
        out_specs=(vmem, vmem, vmem),
        scratch_shapes=[
            pltpu.VMEM(latent.shape, BF16),
            pltpu.VMEM(fresh_noise.shape, BF16),
            pltpu.SMEM(timesteps.shape, jnp.int32),
            pltpu.SMEM(queue_slots.shape, jnp.int32),
            pltpu.SMEM(windows.shape, jnp.int32),
            pltpu.VMEM((Z, T, F, D), BF16),
            pltpu.VMEM((F, T, D), BF16),
            pltpu.VMEM((D, W // 4), BF16),
            pltpu.VMEM((D, W // 2), BF16),
            pltpu.VMEM((D, W // 4), BF16),
            pltpu.VMEM((W // 4, D), BF16),
            pltpu.VMEM(mod_weight.shape, BF16),
            pltpu.VMEM((LAT, D), BF16),
            pltpu.VMEM((2 * F, MP), F32),
            pltpu.VMEM((2 * F, D), F32),
            pltpu.VMEM((F, MP), F32),
            pltpu.VMEM((F, D), F32),
            pltpu.VMEM((2, 8, D), F32),
            pltpu.VMEM((2 * T, D), BF16),
            pltpu.VMEM((F, Z * T, W // 4), BF16),
            pltpu.VMEM((3 * F, Z * T, W // 2), BF16),
            pltpu.VMEM((2 * T, W // 4), BF16),
            pltpu.VMEM((2, 2 * T, D), F32),
            pltpu.VMEM((Z - 1, T, D), BF16),
            pltpu.VMEM((Z - 1, T, D), BF16),
            pltpu.VMEM((Z, T, D), BF16),
            pltpu.VMEM((Z, T, D), BF16),
            pltpu.VMEM((T, LAT), BF16),
            pltpu.VMEM((T, LAT), BF16),
            dma((6,)),
            dma((3 * (W // (4 * HD)),)),
            dma,
            dma,
            dma((Z,)),
            dma((Z,)),
            dma((Z,)),
            dma((Z,)),
            dma((2, Z)),
            dma((2, Z)),
            dma((2, 2, Z)),
            dma((2, 2, Z)),
            dma((2, 2, Z)),
            dma((2, 2, Z)),
            dma,
            dma,
        ],
        compiler_params=pltpu.CompilerParams(
            collective_id=0, has_side_effects=True, vmem_limit_bytes=56 * 1024 * 1024
        ),
        cost_estimate=pl.CostEstimate(
            flops=2 * Z * T * F * D * W, bytes_accessed=2 * D * W, transcendentals=0
        ),
    )(
        hidden,
        latent,
        fresh_noise,
        timesteps,
        queue_slots,
        windows,
        mod_weight,
        attention_weight,
        jnp.transpose(final_weight),
    )
    return pl.pallas_call(
        by_token,
        out_shape=tuple(
            jax.ShapeDtypeStruct((T, F, x.shape[2]), BF16) for x in (out, pred, queue)
        ),
        in_specs=[vmem] * 3,
        out_specs=(vmem,) * 3,
    )(out, pred, queue)


def solution(mesh):
    placed = (
        P("seq", "queue", None),
        P("seq", "queue", None),
        P("seq", None),
        P("queue"),
        P(),
        P(),
        P(None, None, "seq"),
        P(None, "seq"),
        P(),
    )
    return jax.shard_map(
        functools.partial(shards, mesh.shape["queue"], mesh.shape["seq"]),
        mesh=mesh,
        in_specs=placed,
        out_specs=(P("seq", "queue", None), P("seq", "queue", None), P("seq", "queue", None)),
        check_vma=False,
    )
```

```python
import functools
import math

import jax
import jax.numpy as jnp
from jax import lax
from jax.experimental import pallas as pl
from jax.experimental.pallas import tpu as pltpu
from jax.sharding import PartitionSpec as P

HD = 128
STRIDE = 16
WMAX = 2

LN_EPS = 1e-06
DECAY = 2.3
NEAR_COST = 0.5

MESH = pl.DeviceIdType.MESH
F32 = jnp.float32
BF16 = jnp.bfloat16
NT = (((1,), (1,)), ((), ()))


def table(n, values):
    result = values[0]
    for k in range(1, len(values)):
        if values[k] != values[k - 1]:
            result = result + (values[k] - values[k - 1]) * ((n + len(values) - k) // len(values))
    return result


def kernel(
    Q,
    Z,
    hid_hbm,
    lat_hbm,
    fresh_hbm,
    steps_hbm,
    slots_hbm,
    wins_hbm,
    mw_hbm,
    w_hbm,
    fw_hbm,
    out,
    pred,
    queue,
    lat,
    fresh,
    steps,
    slots,
    wins,
    xs,
    own,
    wq,
    wkv,
    wout,
    wout_turned,
    mw,
    fw,
    mod,
    gates_all,
    pattern,
    norm,
    qb,
    kv,
    hd,
    share,
    sent_r,
    sent_l,
    in_r,
    in_l,
    upd,
    got,
    small_sem,
    w_sem,
    mw_sem,
    fw_sem,
    mod_send,
    mod_recv,
    gate_send,
    gate_recv,
    ag_send,
    ag_recv,
    halo_send,
    halo_recv,
    rs_send,
    rs_recv,
    edge_send,
    edge_recv,
):
    T, F, D = hid_hbm.shape
    LH = w_hbm.shape[1] // (4 * HD)
    MP = mw_hbm.shape[2]
    FREQ = mw_hbm.shape[1]
    FRAMES = F * Q
    factor = 1.0 / math.sqrt(HD)
    z = lax.axis_index("seq")
    q = lax.axis_index("queue")
    z_right, z_left = lax.rem(z + 1, Z), lax.rem(z + Z - 1, Z)
    q_right, q_left = lax.rem(q + 1, Q), lax.rem(q + Q - 1, Q)

    def weight_copies():
        copies = []
        for target, first, width in ((wkv, HD, 2 * HD), (wq, 0, HD), (wout, 3 * HD, HD)):
            for h in range(LH):
                copies.append(
                    pltpu.make_async_copy(
                        w_hbm.at[:, pl.ds(h * 4 * HD + first, width)],
                        target.at[:, pl.ds(h * width, width)],
                        w_sem.at[len(copies)],
                    )
                )
        return copies

    barrier = pltpu.get_barrier_semaphore()
    for k in (1, 2, Z - 2, Z - 1):
        pl.semaphore_signal(
            barrier, inc=1, device_id=(q, lax.rem(z + k, Z)), device_id_type=MESH
        )
    for other in (q_left, q_right):
        pl.semaphore_signal(barrier, inc=1, device_id=(other, z), device_id_type=MESH)

    weights = weight_copies()
    small = [
        pltpu.make_async_copy(src, dst, small_sem.at[i])
        for i, (src, dst) in enumerate(
            (
                (steps_hbm, steps),
                (slots_hbm, slots),
                (wins_hbm, wins),
                (lat_hbm, lat),
                (fresh_hbm, fresh),
                (hid_hbm, xs.at[z]),
            )
        )
    ]
    mw_copy = pltpu.make_async_copy(mw_hbm, mw, mw_sem)
    fw_copy = pltpu.make_async_copy(fw_hbm, fw, fw_sem)
    small[0].start()
    mw_copy.start()
    half = T // 2

    def piece(chunk, part_of):
        return xs.at[chunk, pl.ds(part_of * half, half)]

    def gather_copy(way, u, src, chunk, part_of):
        return pltpu.make_async_remote_copy(
            src_ref=src,
            dst_ref=piece(chunk, part_of),
            send_sem=ag_send.at[way, u],
            recv_sem=ag_recv.at[way, u],
            device_id=(q, z_right if way == 0 else z_left),
            device_id_type=MESH,
        )

    def own_copies(u):
        for way in (0, 1):
            part_of = u - 1 if way == 0 else 2 - u
            gather_copy(way, u, hid_hbm.at[pl.ds(part_of * half, half)], z, part_of).start()

    pl.semaphore_wait(barrier, 6)
    own_copies(1)

    small[0].wait()
    rows = lax.broadcasted_iota(jnp.int32, (8, FREQ), 0)
    lanes = lax.broadcasted_iota(jnp.int32, (8, FREQ), 1)
    waves = FREQ // 2
    ladder = jnp.exp(lax.rem(lanes, waves).astype(F32) * (-math.log(10000.0) / waves))
    ids = jnp.where(lax.rem(rows, 2) == 0, steps[0], steps[1])
    angles = ids.astype(F32) * ladder
    freq = jnp.where(lanes < waves, jnp.cos(angles), jnp.sin(angles))
    temb = (freq / (1.0 + jnp.exp(-freq))).astype(BF16)
    mw_copy.wait()
    maps = [jnp.dot(temb, mw[p], preferred_element_type=F32) for p in range(3)]
    rows = lax.broadcasted_iota(jnp.int32, (8, MP), 0)
    pairs = jnp.where(rows < 2, maps[0], maps[1])
    my_columns = pl.ds(pl.multiple_of(z * MP, MP), MP)
    mod[:, my_columns] = pairs[: 2 * F]
    gates_all[:, my_columns] = maps[2][:F]

    def map_copy(i, here, maps_ref, send, recv):
        distance = (1, Z - 1, 2, Z - 2, 1, 2, Z - 1)[i]
        origin = (0, 0, 0, 0, Z - 2, Z - 2, 2)[i]
        owner = lax.rem(z + origin + (0 if here else Z - distance), Z)
        columns = maps_ref.at[:, pl.ds(pl.multiple_of(owner * MP, MP), MP)]
        return pltpu.make_async_remote_copy(
            src_ref=columns,
            dst_ref=columns,
            send_sem=send.at[i],
            recv_sem=recv.at[i],
            device_id=(q, lax.rem(z + distance, Z)),
            device_id_type=MESH,
        )

    def mod_copy(i, here=True):
        return map_copy(i, here, mod, mod_send, mod_recv)

    def gate_copy(i, here=True):
        return map_copy(i, here, gates_all, gate_send, gate_recv)

    def hand_on(copy):
        for i in (2, 3):
            copy(i, False).wait_recv()
        for i in (4, 5, 6):
            copy(i).start()

    for i in range(4):
        mod_copy(i).start()
    own_copies(2)
    for copy in small[1:] + weights + [fw_copy]:
        copy.start()
    in_r[0] = jnp.zeros((T, D), BF16)
    in_l[0] = jnp.zeros((T, D), BF16)

    def choice(rows_count, column_of):
        rows = lax.broadcasted_iota(jnp.int32, (rows_count, rows_count), 0)
        cols = lax.broadcasted_iota(jnp.int32, (rows_count, rows_count), 1)
        return (cols == column_of(rows)).astype(BF16)

    for copy in small[1:]:
        copy.wait()
    by_frame = choice(F * T, lambda r: F * lax.rem(r, T) + lax.div(r, T))
    own_rows = jnp.dot(by_frame, xs[z].reshape(F * T, D), preferred_element_type=F32).astype(BF16)
    for f in range(F):
        own[f] = own_rows[f * T : (f + 1) * T]

    def pass_on(u):
        places = gather_place(u)
        for way in (0, 1):
            chunk, part_of = places[way]
            gather_copy(way, u, piece(chunk, part_of), chunk, part_of).wait_recv()

            @pl.when(u + 2 <= Z - 1)
            def _():
                gather_copy(way, u + 2, piece(chunk, part_of), chunk, part_of).start()

    def gather_place(u):
        step = (u + 1) // 2
        left = (lax.rem(z + Z - step, Z), lax.rem(u + 1, 2))
        right = (lax.rem(z + step, Z), lax.rem(u, 2))
        return left, right

    hand_on(mod_copy)
    pass_on(1)
    pass_on(2)
    for i in (0, 1, 4, 5, 6):
        mod_copy(i, False).wait_recv()
    rows = lax.broadcasted_iota(jnp.int32, (8, D), 0)
    for p in (0, 1):
        pattern[p] = jnp.where(
            lax.rem(rows, 2) == 0, mod[2 * p : 2 * p + 1, :], mod[2 * p + 1 : 2 * p + 2, :]
        ) + float(p)
    for copy in weights:
        copy.wait()
    same = choice(LH * HD, lambda r: r)
    tile = 512
    for c in range(0, D, tile):
        wout_turned[:, c : c + tile] = lax.dot_general(
            same, wout[c : c + tile, :], NT, preferred_element_type=F32
        ).astype(BF16)

    def normalise(chunk, part_of, base):
        for r in range(0, half, 8):
            x = xs[chunk, pl.ds(part_of * half + r, 8)].reshape(16, D).astype(F32)
            centred = x - jnp.sum(x, axis=1, keepdims=True) * (1.0 / D)
            variance = jnp.sum(centred * centred, axis=1, keepdims=True) * (1.0 / D)
            y = (centred * lax.rsqrt(variance + LN_EPS)).reshape(2, 8, D)
            y = y * pattern[1][None] + pattern[0][None]
            norm[base + F * r : base + F * r + 16, :] = y.reshape(16, D).astype(BF16)

    def token_rows(chunk, part_of):
        return pl.ds(pl.multiple_of(chunk * T + part_of * half, half), half)

    def halo_copy(side, u, i, chunk, part_of):
        rows_here = token_rows(chunk, part_of)
        return pltpu.make_async_remote_copy(
            src_ref=kv.at[pl.ds(F, F), rows_here],
            dst_ref=kv.at[pl.ds(0 if side == 0 else 2 * F, F), rows_here],
            send_sem=halo_send.at[side, i, u],
            recv_sem=halo_recv.at[side, i, u],
            device_id=(q_right if side == 0 else q_left, z),
            device_id_type=MESH,
        )

    split = choice(
        2 * T,
        lambda r: lax.rem(lax.div(r, half), 2) * T + F * lax.rem(r, half) + lax.div(r, T),
    )

    def halo_wait(u):
        places = gather_place(u)
        for way in (0, 1):
            for side in (0, 1):
                halo_copy(side, u, way, *places[way]).wait_recv()

    def project(weight):
        mixed_rows = jnp.dot(norm[...], weight[...], preferred_element_type=F32).astype(BF16)
        return jnp.dot(split, mixed_rows, preferred_element_type=F32).astype(BF16)

    def keep_queries(u):
        places = gather_place(u)
        projected = project(wq)
        for way in (0, 1):
            rows_here = token_rows(*places[way])
            for f in range(F):
                at_row = f * T + way * half
                qb[f, rows_here, :] = projected[at_row : at_row + half]

    def gather_unit(u, carry):
        places = gather_place(u)
        pl.when(u >= 3)(lambda: pass_on(u))

        for way in (0, 1):
            normalise(*places[way], way * T)
        projected = project(wkv)
        for way in (0, 1):
            rows_here = token_rows(*places[way])
            for f in range(F):
                at_row = f * T + way * half
                kv[F + f, rows_here, :] = projected[at_row : at_row + half]
            for side in (0, 1):
                halo_copy(side, u, way, *places[way]).start()

        @pl.when(u < Z - 1)
        def _():
            keep_queries(u)

        @pl.when(u >= 2)
        def _():
            halo_wait(u - 2)

        return carry

    lax.fori_loop(0, Z, gather_unit, 0)
    for i in range(4):
        gate_copy(i).start()

    def spatial(pieces):
        each = [(chunk, frame, h) for chunk, frame in pieces for h in range(LH)]
        scores = [
            lax.dot_general(
                qb[frame, pl.ds(pl.multiple_of(chunk * T, T), T), h * HD : (h + 1) * HD],
                kv[F + frame, :, h * 2 * HD : h * 2 * HD + HD],
                NT,
                preferred_element_type=F32,
            )
            for chunk, frame, h in each
        ]
        scores = [score * factor for score in scores]
        peaks = [jnp.max(score, axis=1, keepdims=True) for score in scores]
        expos = [jnp.exp(score - peak) for score, peak in zip(scores, peaks)]
        totals = [jnp.sum(expo, axis=1, keepdims=True) for expo in expos]
        mixed = [
            jnp.dot(
                expo.astype(BF16),
                kv[F + frame, :, h * 2 * HD + HD : (h + 1) * 2 * HD],
                preferred_element_type=F32,
            )
            for expo, (chunk, frame, h) in zip(expos, each)
        ]
        results = [m / total for m, total in zip(mixed, totals)]
        return [results[:LH], results[LH:]]

    def temporal(chunk, frame):
        rows_here = pl.ds(pl.multiple_of(chunk * T, T), T)
        here = q * F + frame
        slot = slots[here]
        window = wins[here]
        gates = []
        for d in range(-WMAX, WMAX + 1):
            there = here + d
            inside = jnp.logical_and(there >= 0, there < FRAMES)
            gap = jnp.abs(slots[jnp.clip(there, 0, FRAMES - 1)] - slot)
            gates.append((jnp.logical_and(inside, gap <= window), gap.astype(F32) * NEAR_COST))
        results = []
        for h in range(LH):
            queries = qb[frame, rows_here, h * HD : (h + 1) * HD].astype(F32)
            logits = []
            for d in range(2 * WMAX + 1):
                keys = kv[F + frame + d - WMAX, rows_here, h * 2 * HD : h * 2 * HD + HD]
                score = jnp.sum(queries * keys.astype(F32), axis=1, keepdims=True) * factor
                allowed, cost = gates[d]
                logits.append(jnp.where(allowed, score - cost, -1e30))
            peak = functools.reduce(jnp.maximum, logits)
            total = jnp.zeros((T, 1), F32)
            mixed = jnp.zeros((T, HD), F32)
            for d in range(2 * WMAX + 1):
                weight = jnp.where(gates[d][0], jnp.exp(logits[d] - peak), 0.0)
                values = kv[
                    F + frame + d - WMAX, rows_here, h * 2 * HD + HD : (h + 1) * 2 * HD
                ]
                total = total + weight
                mixed = mixed + weight * values.astype(F32)
            results.append(mixed / total)
        return results

    def scatter_copy(way, n, part_of):
        src, dst = (sent_r, in_r) if way == 0 else (sent_l, in_l)
        rows_here = pl.ds(part_of * half, half)
        return pltpu.make_async_remote_copy(
            src_ref=src.at[n - 1, rows_here],
            dst_ref=dst.at[n, rows_here],
            send_sem=rs_send.at[way, part_of, n],
            recv_sem=rs_recv.at[way, part_of, n],
            device_id=(q, z_right if way == 0 else z_left),
            device_id_type=MESH,
        )

    def drain(u, carry):
        places = gather_place(u)
        for way in (0, 1):

            @pl.when(u >= 1)
            def _():
                gather_copy(way, u, piece(*places[way]), *places[way]).wait_send()

            for side in (0, 1):
                halo_copy(side, u, way, *places[way]).wait_send()
        return carry

    def sent_off(n, carry):
        for way in (0, 1):
            for part_of in (0, 1):
                scatter_copy(way, n, part_of).wait_send()
        return carry

    own_turn = Z // 2

    def scatter_unit(m, carry):
        n = table(m, (0, 1, 2, 3, 0, 4, 5, 6, 7))
        right_step = table(m, (0, 3, 4, 2, 0, 3, 2, 1, 1))
        left_step = table(m, (0, 3, 4, 2, 0, 3, 1, 2, 1))
        right = (lax.rem(z + right_step, Z), table(m, (1, 1, 0, 1, 1, 0, 0, 0, 1)))
        left = (lax.rem(z + Z - left_step, Z), table(m, (0, 0, 1, 0, 0, 1, 0, 1, 1)))
        place = table(m, (0, 0, 0, 0, 1, 0, 0, 0, 0))

        @pl.when(m == 2)
        def _():
            keep_queries(Z - 1)

        spread = spatial([right, left])

        @pl.when(m == 1)
        def _():
            halo_wait(Z - 2)

        @pl.when(m == 2)
        def _():
            halo_wait(Z - 1)

        along = [temporal(*right), temporal(*left)]
        for i in (0, 1):
            for h in range(LH):
                hd[i * T : (i + 1) * T, h * HD : (h + 1) * HD] = (
                    spread[i][h] + along[i][h]
                ).astype(BF16)
        for c in range(0, D, tile):
            share[place, :, c : c + tile] = jnp.dot(
                hd[...], wout_turned[:, c : c + tile], preferred_element_type=F32
            )

        @pl.when(m != own_turn)
        def _():
            needs = (
                table(m, (0, 0, 0, 1, 0, 2, 4, 5, 3)),
                table(m, (0, 0, 0, 1, 0, 2, 3, 4, 6)),
            )
            for part_of in (0, 1):
                for way, (sent, arrived) in enumerate(((sent_r, in_r), (sent_l, in_l))):
                    need = needs[way]

                    @pl.when(m >= 3)
                    def _():
                        scatter_copy(way, need, part_of).wait_recv()

                    mine = way * T + part_of * half
                    rows_here = slice(part_of * half, (part_of + 1) * half)
                    sent[n - 1, rows_here, :] = (
                        share[0, mine : mine + half, :]
                        + arrived[need, rows_here, :].astype(F32)
                    ).astype(BF16)
                    scatter_copy(way, n, part_of).start()

        @pl.when(m == own_turn)
        def _():
            hand_on(gate_copy)
            lax.fori_loop(0, Z, drain, 0)

        return carry

    lax.fori_loop(1, Z + 1, scatter_unit, 0)

    lax.fori_loop(1, Z - 2, sent_off, 0)
    fw_copy.wait()
    for i in (0, 1, 4, 5, 6):
        gate_copy(i, False).wait_recv()
    for i in range(7):
        gate_copy(i).wait_send()
        mod_copy(i).wait_send()
    horizon = STRIDE * (FRAMES + 1)
    LAT = lat.shape[2]

    def schedule(f):
        ids = jnp.full((T, LAT), steps[f], jnp.int32)
        now = jnp.exp(ids.astype(F32) * (-DECAY / horizon))
        before = jnp.exp((ids - STRIDE).astype(F32) * (-DECAY / horizon))
        return jnp.sqrt(1.0 - now), jnp.sqrt(now), jnp.sqrt(before), jnp.sqrt(1.0 - before)

    tables = [schedule(f) for f in range(F)]
    edge = pltpu.make_async_remote_copy(
        src_ref=upd,
        dst_ref=got,
        send_sem=edge_send,
        recv_sem=edge_recv,
        device_id=(q_left, z),
        device_id_type=MESH,
    )
    last = ((6, 5), (7, 7))
    for f in range(F):
        for way in (0, 1):
            for part_of in (0, 1):
                scatter_copy(way, last[f][way], part_of).wait_recv()
        mine = (1 - f) * T
        total = (
            share[1, mine : mine + T, :]
            + in_r[last[f][0]].astype(F32)
            + in_l[last[f][1]].astype(F32)
        )
        gate = gates_all[f : f + 1, :]
        block = (own[f].astype(F32) + gate * total).astype(BF16)
        out[f] = block
        noise = lax.dot_general(block, fw[...], NT, preferred_element_type=F32)
        pred[f] = noise.astype(BF16)
        noise_now, root_now, root_before, noise_before = tables[f]
        clean = (lat[:, f, :].astype(F32) - noise_now * noise) / root_now
        updated = (root_before * clean + noise_before * noise).astype(BF16)
        if f == 0:
            upd[...] = updated
            edge.start()
        else:
            queue[f - 1] = updated
    edge.wait_recv()
    queue[F - 1] = jnp.where(q == Q - 1, fresh[...], got[...])

    edge.wait_send()
    lax.fori_loop(Z - 2, Z, sent_off, 0)


def by_token(*refs):
    for src, dst in zip(refs[:3], refs[3:]):
        for f in range(src.shape[0]):
            dst[:, f, :] = src[f]


def shards(
    Q,
    Z,
    hidden,
    latent,
    fresh_noise,
    timesteps,
    queue_slots,
    windows,
    mod_weight,
    attention_weight,
    final_weight,
):
    T, F, D = hidden.shape
    LAT = latent.shape[2]
    W = attention_weight.shape[1]
    MP = mod_weight.shape[2]
    vmem = pl.BlockSpec(memory_space=pltpu.VMEM)
    hbm = pl.BlockSpec(memory_space=pltpu.HBM)
    dma = pltpu.SemaphoreType.DMA
    out, pred, queue = pl.pallas_call(
        functools.partial(kernel, Q, Z),
        out_shape=(
            jax.ShapeDtypeStruct((F, T, D), BF16),
            jax.ShapeDtypeStruct((F, T, LAT), BF16),
            jax.ShapeDtypeStruct((F, T, LAT), BF16),
        ),
        in_specs=[hbm] * 9,
        out_specs=(vmem, vmem, vmem),
        scratch_shapes=[
            pltpu.VMEM(latent.shape, BF16),
            pltpu.VMEM(fresh_noise.shape, BF16),
            pltpu.SMEM(timesteps.shape, jnp.int32),
            pltpu.SMEM(queue_slots.shape, jnp.int32),
            pltpu.SMEM(windows.shape, jnp.int32),
            pltpu.VMEM((Z, T, F, D), BF16),
            pltpu.VMEM((F, T, D), BF16),
            pltpu.VMEM((D, W // 4), BF16),
            pltpu.VMEM((D, W // 2), BF16),
            pltpu.VMEM((D, W // 4), BF16),
            pltpu.VMEM((W // 4, D), BF16),
            pltpu.VMEM(mod_weight.shape, BF16),
            pltpu.VMEM((LAT, D), BF16),
            pltpu.VMEM((2 * F, D), F32),
            pltpu.VMEM((F, D), F32),
            pltpu.VMEM((2, 8, D), F32),
            pltpu.VMEM((2 * T, D), BF16),
            pltpu.VMEM((F, Z * T, W // 4), BF16),
            pltpu.VMEM((3 * F, Z * T, W // 2), BF16),
            pltpu.VMEM((2 * T, W // 4), BF16),
            pltpu.VMEM((2, 2 * T, D), F32),
            pltpu.VMEM((Z - 1, T, D), BF16),
            pltpu.VMEM((Z - 1, T, D), BF16),
            pltpu.VMEM((Z, T, D), BF16),
            pltpu.VMEM((Z, T, D), BF16),
            pltpu.VMEM((T, LAT), BF16),
            pltpu.VMEM((T, LAT), BF16),
            dma((6,)),
            dma((3 * (W // (4 * HD)),)),
            dma,
            dma,
            dma((Z,)),
            dma((Z,)),
            dma((Z,)),
            dma((Z,)),
            dma((2, Z)),
            dma((2, Z)),
            dma((2, 2, Z)),
            dma((2, 2, Z)),
            dma((2, 2, Z)),
            dma((2, 2, Z)),
            dma,
            dma,
        ],
        compiler_params=pltpu.CompilerParams(
            collective_id=0, has_side_effects=True, vmem_limit_bytes=56 * 1024 * 1024
        ),
        cost_estimate=pl.CostEstimate(
            flops=2 * Z * T * F * D * W, bytes_accessed=2 * D * W, transcendentals=0
        ),
    )(
        hidden,
        latent,
        fresh_noise,
        timesteps,
        queue_slots,
        windows,
        mod_weight,
        attention_weight,
        jnp.transpose(final_weight),
    )
    return pl.pallas_call(
        by_token,
        out_shape=tuple(
            jax.ShapeDtypeStruct((T, F, x.shape[2]), BF16) for x in (out, pred, queue)
        ),
        in_specs=[vmem] * 3,
        out_specs=(vmem,) * 3,
    )(out, pred, queue)


def solution(mesh):
    placed = (
        P("seq", "queue", None),
        P("seq", "queue", None),
        P("seq", None),
        P("queue"),
        P(),
        P(),
        P(None, None, "seq"),
        P(None, "seq"),
        P(),
    )
    return jax.shard_map(
        functools.partial(shards, mesh.shape["queue"], mesh.shape["seq"]),
        mesh=mesh,
        in_specs=placed,
        out_specs=(P("seq", "queue", None), P("seq", "queue", None), P("seq", "queue", None)),
        check_vma=False,
    )
```
